512 devices in a mesh: tm: 32 (over y_lo, z), dp: 16 (over x, y_hi, core).
Axes of the slice: x: 4, y: 8 (y_hi: 2, y_lo: 4; y = y_hi * 4 + y_lo), z: 8, core: 2. Of those that a mesh axis runs over, the one named last changes fastest.
Arguments:
- query_raw: bfloat16 [16, 4096, 1536], P('dp', 'tm'), may hold values from -500 to 500
- key_raw: bfloat16 [16, 4096, 1536], P('dp', 'tm'), may hold values from -500 to 500
- value_rows: bfloat16 [16, 4096, 1536], P('dp', 'tm'), may hold values from -6 to 6
- grad_output: bfloat16 [16, 4096, 1536], P('dp', 'tm'), may hold values from -1200 to 1200
- log_normalizer: float32 [16, 12, 4096], P('dp', None, 'tm'), may hold values from 6 to 8
- output_dot: float32 [16, 12, 4096], P('dp', None, 'tm'), may hold values from -384 to 384
- query_gain: float32 [128], replicated, may hold values from 0.1 to 1.9
- key_gain: float32 [128], replicated, may hold values from 0.1 to 1.9
- route_blocks: int32 [16, 32, 2], P('dp'), may hold values from 0 to 2, as said below
- route_count: int32 [16, 32], P('dp'), may hold values from 1 to 2, as said below
- query_reach: int32 [16, 64], P('dp'), may hold values from 1 to 12, as said below
Outputs:
- query_grad: bfloat16 [16, 4096, 1536], P('dp', 'tm')
- key_grad: bfloat16 [16, 4096, 1536], P('dp', 'tm')
- value_grad: bfloat16 [16, 4096, 1536], P('dp', 'tm')
- query_gain_grad: float32 [128], replicated
- key_gain_grad: float32 [128], replicated
The draws below stay inside these ranges and needn't reach their ends.
Inputs may be any that keep to these rules, and one draw needn't show every extreme that they name: `route_blocks`: for each clip and shard, 2 different blocks of the shard; only the first route_count of them are routed. `route_count`: in every clip some shard routes 2 blocks. `query_reach`: in every clip some slot block has reach 12.
All inputs are finite; a program needn't handle non-finite values.
Results may differ from the reference program's by a relative error of at most 0.0083.
Values may be sent and summed in bfloat16 or wider, within the bound.
No kernel may reach another device: no remote copies, remote signals or barrier semaphores. Data moves between devices by JAX's collectives and lax.ppermute only.
A program may use at most 64 MiB of HBM per device.

```python
import jax
import jax.numpy as jnp
from jax import lax

HEADS = 12
HEAD_DIM = 128
BLK = 64
NBLK = 3
ROUTE_MOST = 2
STEPS = 4
HD = 1536
CAP = 128
REACH = 12
CLIPS = 16
N_TM = 32
N_DP = 16


def spread_scales(scale_key, upper):
    row_key, column_key = jax.random.split(scale_key)
    row_scales = jnp.exp(jax.random.uniform(row_key, (CLIPS, N_TM * CAP, HEADS, 1), jnp.float32) * jnp.log(upper))
    column_scales = jnp.exp(jax.random.uniform(column_key, (HEAD_DIM,), jnp.float32) * jnp.log(upper))
    return row_scales * column_scales


def draw_query_raw(key, part):
    key = jax.random.fold_in(key, 11)
    base_key, scale_key = jax.random.split(key)
    full_shape = (CLIPS, N_TM * CAP, HEADS, HEAD_DIM)
    base_draw = jnp.clip(jax.random.normal(base_key, full_shape, jnp.float32), -5.0, 5.0)
    spread = spread_scales(scale_key, 10.0)
    return (base_draw * spread).reshape(CLIPS, N_TM * CAP, HEADS * HEAD_DIM).astype(jnp.bfloat16)


def draw_key_raw(key, part):
    key = jax.random.fold_in(key, 12)
    base_key, scale_key = jax.random.split(key)
    full_shape = (CLIPS, N_TM * CAP, HEADS, HEAD_DIM)
    base_draw = jnp.clip(jax.random.normal(base_key, full_shape, jnp.float32), -5.0, 5.0)
    spread = spread_scales(scale_key, 10.0)
    return (base_draw * spread).reshape(CLIPS, N_TM * CAP, HEADS * HEAD_DIM).astype(jnp.bfloat16)


def draw_grad_output(key, part):
    key = jax.random.fold_in(key, 13)
    full_shape = (CLIPS, N_TM * CAP, HEADS * HEAD_DIM)
    along_rows = jnp.arange(N_TM * CAP, dtype=jnp.float32)[None, :, None] / (N_TM * CAP - 1)
    across = jnp.arange(CLIPS, dtype=jnp.float32)[:, None, None] / max(CLIPS - 1, 1)
    base_draw = jnp.clip(jax.random.normal(key, full_shape, jnp.float32), -5.0, 5.0)
    rise_factor = jnp.exp((along_rows + across) * jnp.log(3.0))
    return (8.0 * base_draw * rise_factor).astype(jnp.bfloat16)


def shard_order(order_key):
    return jax.random.permutation(order_key, NBLK)


def route_tables(key):
    count_key, pick_key, block_key = jax.random.split(key, 3)
    counts = jax.random.randint(count_key, (CLIPS, N_TM), 1, ROUTE_MOST + 1)
    chosen = jax.random.randint(pick_key, (CLIPS, 1), 0, N_TM)
    counts = jnp.where(jnp.arange(N_TM)[None, :] == chosen, ROUTE_MOST, counts)
    orders = jax.vmap(shard_order)(jax.random.split(block_key, CLIPS * N_TM))
    blocks = orders[:, :ROUTE_MOST].reshape(CLIPS, N_TM, ROUTE_MOST)
    return (blocks.astype(jnp.int32), counts.astype(jnp.int32))


def draw_route_blocks(key, part):
    shared = route_tables(key)
    return shared[0]


def draw_route_count(key, part):
    shared = route_tables(key)
    return shared[1]


def draw_query_reach(key, part):
    key = jax.random.fold_in(key, 19)
    value_key, pick_key = jax.random.split(key)
    reaches = jax.random.randint(value_key, (CLIPS, N_TM * ROUTE_MOST), 1, REACH + 1)
    chosen = jax.random.randint(pick_key, (CLIPS, 1), 0, N_TM * ROUTE_MOST)
    return jnp.where(jnp.arange(N_TM * ROUTE_MOST)[None, :] == chosen, REACH, reaches).astype(jnp.int32)


def block_scale(own_key, shape, shards, least, top_value):
    level = 1.0
    for axis_at, parts in shards:
        heights = jax.random.uniform(jax.random.fold_in(jax.random.fold_in(own_key, 6), axis_at), (parts,), jnp.float32, least / len(shards), top_value / len(shards))
        level = level * jnp.repeat(jnp.exp(heights), shape[axis_at] // parts).reshape((-1,) + (1,) * (len(shape) - 1 - axis_at))
    return level


def gaussian(rng, dims, scale, reach, cuts=(), held_as=jnp.bfloat16):
    factor_of = block_scale(rng, dims, cuts, -0.22, 0.18) if cuts else 1.0
    entries = jax.random.normal(rng, dims, jnp.float32) * scale * factor_of
    return jnp.minimum(jnp.maximum(entries, -reach), reach).astype(held_as)


def setup_inputs(seed: int = 0) -> dict:
    arg_keys = jax.random.split(jax.random.key(seed), 12)
    return {
        "query_raw": draw_query_raw(jax.random.fold_in(arg_keys[11], 71), 0),
        "key_raw": draw_key_raw(jax.random.fold_in(arg_keys[11], 71), 0),
        "value_rows": gaussian(arg_keys[2], (CLIPS, N_TM * CAP, HD), 1.0, 6.0, ((0, 16), (1, 32))),
        "grad_output": draw_grad_output(jax.random.fold_in(arg_keys[11], 71), 0),
        "log_normalizer": jnp.clip(6.0 + 2.0 * jax.random.uniform(arg_keys[4], (CLIPS, HEADS, N_TM * CAP), jnp.float32) ** block_scale(arg_keys[4], (CLIPS, HEADS, N_TM * CAP), ((0, 16), (2, 32)), -0.2, 0.2), 6.0, 8.0),
        "output_dot": gaussian(arg_keys[5], (CLIPS, HEADS, N_TM * CAP), 60.0, 384.0, ((0, 16), (2, 32)), jnp.float32),
        "query_gain": jnp.clip(1.0 + 0.18 * jax.random.normal(arg_keys[6], (HEAD_DIM,), jnp.float32), 0.1, 1.9),
        "key_gain": jnp.clip(1.0 + 0.18 * jax.random.normal(arg_keys[7], (HEAD_DIM,), jnp.float32), 0.1, 1.9),
        "route_blocks": draw_route_blocks(jax.random.fold_in(arg_keys[11], 71), 0),
        "route_count": draw_route_count(jax.random.fold_in(arg_keys[11], 71), 0),
        "query_reach": draw_query_reach(jax.random.fold_in(arg_keys[11], 71), 0),
    }


norm_eps = 1e-06

def prepare(raw_heads, gain_vector):
    widened = raw_heads.astype(jnp.float32)
    inverse = lax.rsqrt(lax.optimization_barrier(jnp.mean(widened * widened, axis=-1, keepdims=True)) + norm_eps)
    normal_unit = widened * inverse
    return (normal_unit, inverse, (normal_unit * gain_vector).astype(jnp.bfloat16))

def norm_back(grad_normed, normal_unit, inverse, gain_vector):
    scaled = grad_normed * gain_vector
    grad_raw = inverse * (scaled - normal_unit * lax.optimization_barrier(jnp.mean(scaled * normal_unit, axis=-1, keepdims=True)))
    summed_axes = tuple(range(normal_unit.ndim - 1))
    return (grad_raw, lax.optimization_barrier(jnp.sum(grad_normed * normal_unit, axis=summed_axes)))

def allowed_pairs(tables, query_src, key_src, offset):
    blocks, counts, reaches = tables
    slot_index = jnp.arange(ROUTE_MOST * BLK, dtype=jnp.int32)
    query_blocks = jnp.repeat(lax.dynamic_index_in_dim(blocks, query_src, 0, False), BLK)
    key_blocks = jnp.repeat(lax.dynamic_index_in_dim(blocks, key_src, 0, False), BLK)
    reach_rows = jnp.repeat(lax.dynamic_slice_in_dim(reaches, query_src * ROUTE_MOST, ROUTE_MOST), BLK)
    query_live = slot_index < lax.dynamic_index_in_dim(counts, query_src, 0, False) * BLK
    key_live = slot_index < lax.dynamic_index_in_dim(counts, key_src, 0, False) * BLK
    within_reach = offset * NBLK + query_blocks[:, None] - key_blocks[None, :] < reach_rows[:, None]
    return query_live[:, None] & key_live[None, :] & within_reach

def pair_terms(query_normed, output_heads, log_rows, dot_rows, key_normed, value_heads, allowed):
    score_scale = HEAD_DIM ** (-0.5)
    scores = jnp.einsum('qhd,khd->hqk', query_normed.astype(jnp.float32), key_normed.astype(jnp.float32)) * score_scale
    probability = jnp.where(allowed[None], jnp.exp(scores - log_rows[:, :, None]), 0.0)
    weights_low = lax.optimization_barrier(probability.astype(jnp.bfloat16))
    grad_values = jnp.einsum('hqk,qhd->khd', weights_low.astype(jnp.float32), output_heads.astype(jnp.float32))
    grad_weights = jnp.einsum('qhd,khd->hqk', output_heads.astype(jnp.float32), value_heads.astype(jnp.float32))
    grad_scores = lax.optimization_barrier((probability * (grad_weights - dot_rows[:, :, None])).astype(jnp.bfloat16))
    grad_scores = grad_scores.astype(jnp.float32)
    grad_query = jnp.einsum('hqk,khd->qhd', grad_scores, key_normed.astype(jnp.float32)) * score_scale
    grad_key = jnp.einsum('hqk,qhd->khd', grad_scores, query_normed.astype(jnp.float32)) * score_scale
    return (grad_query, grad_key, grad_values)

def add_block(running, position, addition):
    current = lax.dynamic_index_in_dim(running, position, 0, False)
    return lax.dynamic_update_index_in_dim(running, current + addition, position, 0)

def reference(query_raw, key_raw, value_rows, grad_output, log_normalizer, output_dot, query_gain, key_gain, route_blocks, route_count, query_reach):
    head_shape = (N_TM, CAP, HEADS, HEAD_DIM)
    flat_shape = (N_TM * CAP, HEADS * HEAD_DIM)

    def one_clip(clip_args):
        query_clip, key_clip, value_clip, output_clip, log_clip, dot_clip, blocks, counts, reaches = clip_args
        tables = (blocks, counts, reaches)
        query_unit, query_inverse, query_normed = prepare(query_clip.reshape(head_shape), query_gain)
        key_unit, key_inverse, key_normed = prepare(key_clip.reshape(head_shape), key_gain)
        value_heads = value_clip.reshape(head_shape)
        output_heads = output_clip.reshape(head_shape)
        log_rows = log_clip.reshape(HEADS, N_TM, CAP)
        dot_rows = dot_clip.reshape(HEADS, N_TM, CAP)

        def per_shard(carried, shard_here):
            key_total, value_total = carried
            query_here = lax.dynamic_index_in_dim(query_normed, shard_here, 0, False)
            output_here = lax.dynamic_index_in_dim(output_heads, shard_here, 0, False)
            log_here = lax.dynamic_index_in_dim(log_rows, shard_here, 1, False)
            dot_here = lax.dynamic_index_in_dim(dot_rows, shard_here, 1, False)
            query_total = jnp.zeros((CAP, HEADS, HEAD_DIM), jnp.float32)
            for offset in range(STEPS):
                source = ((shard_here - offset) % N_TM).astype(jnp.int32)
                allowed = allowed_pairs(tables, shard_here, source, offset)
                query_part, key_part, value_part = pair_terms(query_here, output_here, log_here, dot_here, lax.dynamic_index_in_dim(key_normed, source, 0, False), lax.dynamic_index_in_dim(value_heads, source, 0, False), allowed)
                query_total = query_total + query_part
                key_total = add_block(key_total, source, key_part)
                value_total = add_block(value_total, source, value_part)
            return ((key_total, value_total), query_total)
        zeros_acc = jnp.zeros(head_shape, jnp.float32)
        (key_total, value_total), query_total = lax.scan(per_shard, (zeros_acc, zeros_acc), jnp.arange(N_TM, dtype=jnp.int32))
        query_grad, query_term = norm_back(query_total, query_unit, query_inverse, query_gain)
        key_grad, key_term = norm_back(key_total, key_unit, key_inverse, key_gain)
        return (query_grad.reshape(flat_shape).astype(jnp.bfloat16), key_grad.reshape(flat_shape).astype(jnp.bfloat16), value_total.reshape(flat_shape).astype(jnp.bfloat16), query_term, key_term)
    results = lax.map(one_clip, (query_raw, key_raw, value_rows, grad_output, log_normalizer, output_dot, route_blocks, route_count, query_reach))
    divisor = N_TM * N_DP
    return (results[0], results[1], results[2], lax.optimization_barrier(jnp.sum(results[3], axis=0)) / divisor, lax.optimization_barrier(jnp.sum(results[4], axis=0)) / divisor)
```

```python
import functools

import jax
import jax.numpy as jnp
from jax import lax
from jax.experimental import pallas as pl
from jax.experimental.pallas import tpu as pltpu
from jax.sharding import PartitionSpec as P

BLK = 64
NBLK = 3
ROUTE_MOST = 2
STEPS = 4
HEADS = 12
WIDTH = 128
CAP = ROUTE_MOST * BLK
HD = HEADS * WIDTH
STAT_ROWS = 16
LOG2E = 1.4426950408889634
SCALE = WIDTH**-0.5
CLOSED = -1e30
norm_eps = 1e-06

f32 = jnp.float32
bf16 = jnp.bfloat16


def head_lanes(h):
    return pl.ds(pl.multiple_of(h * WIDTH, WIDTH), WIDTH)


def over_heads(step, unroll=2):
    lax.fori_loop(0, HEADS, lambda h, none: step(h), None, unroll=unroll)


def unit_of(raw):
    widened = raw.astype(f32)
    inverse = lax.rsqrt(jnp.mean(widened * widened, axis=-1, keepdims=True) + norm_eps)
    return widened * inverse, inverse


def three_parts(row):
    high = row.astype(bf16)
    rest = row - high.astype(f32)
    middle = rest.astype(bf16)
    low = (rest - middle.astype(f32)).astype(bf16)
    return high, middle, low


def prep_kernel(
    blocks_ref, counts_ref, reach_ref, query_ref, key_ref, log_ref, dot_ref, qgain_ref, kgain_ref,
    qx_ref, kn_ref, bias_ref,
):
    shards = counts_ref.shape[1]
    here = lax.axis_index("tm")
    lane = lax.broadcasted_iota(jnp.int32, (1, CAP), 1)

    def pair_rows(query_shard, key_shard, offset):
        rows = []
        for kj in range(ROUTE_MOST):
            values = []
            for qi in range(ROUTE_MOST):
                near = (
                    offset * NBLK
                    + blocks_ref[0, query_shard, qi]
                    - blocks_ref[0, key_shard, kj]
                    < reach_ref[0, query_shard * ROUTE_MOST + qi]
                )
                live = (qi < counts_ref[0, query_shard]) & (kj < counts_ref[0, key_shard])
                values.append(jnp.where(near & live, 0.0, CLOSED).astype(f32))
            rows.append(jnp.where(lane < BLK, values[0], values[1]))
        return rows

    rows = []
    for offset in range(STEPS):
        rows += pair_rows(here, lax.rem(here - offset + shards, shards), offset)
    for offset in range(1, STEPS):
        rows += pair_rows(lax.rem(here + offset, shards), here, offset)
    for at, row in enumerate(rows):
        bias_ref[at : at + 1, :] = row
    bias_ref[len(rows) :, :] = jnp.zeros((bias_ref.shape[0] - len(rows), CAP), f32)

    def one_head(h):
        lanes = head_lanes(h)
        unit, _ = unit_of(query_ref[:, lanes])
        qx_ref[:CAP, lanes] = (unit * qgain_ref[...]).astype(bf16)
        unit, _ = unit_of(key_ref[:, lanes])
        kn_ref[:, lanes] = (unit * kgain_ref[...]).astype(bf16)
        log_row = log_ref[pl.ds(h, 1), :] * -LOG2E
        dot_row = dot_ref[pl.ds(h, 1), :]
        parts = [p.astype(f32) for p in three_parts(log_row) + three_parts(dot_row)]
        parts.append(jnp.zeros((STAT_ROWS - len(parts), CAP), f32))
        qx_ref[CAP:, lanes] = jnp.concatenate(parts, axis=0).astype(bf16)

    over_heads(one_head)


def stat_rows(qx_ref, lanes):
    stats = qx_ref[CAP:, lanes].astype(f32)
    log_row = stats[0:1] + stats[1:2] + stats[2:3]
    dot_row = stats[3:4] + stats[4:5] + stats[5:6]
    return log_row, dot_row


def dot_nt(a, b):
    return lax.dot_general(a, b, (((1,), (1,)), ((), ())), preferred_element_type=f32)


def dot_nn(a, b):
    return lax.dot_general(a, b, (((1,), (0,)), ((), ())), preferred_element_type=f32)


def dot_tn(a, b):
    return lax.dot_general(a, b, (((0,), (0,)), ((), ())), preferred_element_type=f32)


def pair_core(qx_ref, do_ref, kn_ref, v_ref, bias_ref, at, lanes):
    log_row, dot_row = stat_rows(qx_ref, lanes)
    scores = dot_nt(kn_ref[:, lanes], qx_ref[:CAP, lanes])
    half = [
        jnp.exp2(
            scores[j * BLK : (j + 1) * BLK] * (SCALE * LOG2E)
            + (log_row + bias_ref[at + j : at + j + 1, :])
        )
        for j in range(ROUTE_MOST)
    ]
    probability = jnp.concatenate(half, axis=0)
    grad_weights = dot_nt(v_ref[:, lanes], do_ref[:, lanes])
    grad_scores = (probability * (grad_weights - dot_row)).astype(bf16)
    return probability.astype(bf16), grad_scores


def own_kernel(qx_ref, do_ref, kn_ref, v_ref, bias_ref, dq_ref, dk_ref, dv_ref):
    def one_head(h):
        lanes = head_lanes(h)
        weights, grad_scores = pair_core(qx_ref, do_ref, kn_ref, v_ref, bias_ref, 0, lanes)
        dq_ref[:, lanes] = dot_tn(grad_scores, kn_ref[:, lanes])
        dk_ref[:, lanes] = dot_nn(grad_scores, qx_ref[:CAP, lanes])
        dv_ref[:, lanes] = dot_nn(weights, do_ref[:, lanes])

    over_heads(one_head)


def step_kernel(
    offset,
    qx_ref, do_ref, kn_ref, v_ref, far_qx_ref, far_do_ref, far_kn_ref, far_v_ref, bias_ref,
    dq_in, dk_in, dv_in, dq_ref, dk_ref, dv_ref,
):
    def one_head(h):
        lanes = head_lanes(h)
        _, grad_scores = pair_core(
            qx_ref, do_ref, far_kn_ref, far_v_ref, bias_ref, offset * ROUTE_MOST, lanes
        )
        dq_ref[:, lanes] = dq_in[:, lanes] + dot_tn(grad_scores, far_kn_ref[:, lanes])
        weights, grad_scores = pair_core(
            far_qx_ref, far_do_ref, kn_ref, v_ref, bias_ref, (STEPS - 1 + offset) * ROUTE_MOST, lanes
        )
        dk_ref[:, lanes] = dk_in[:, lanes] + dot_nn(grad_scores, far_qx_ref[:CAP, lanes])
        dv_ref[:, lanes] = dv_in[:, lanes] + dot_nn(weights, far_do_ref[:, lanes])

    over_heads(one_head)


def norm_back(total, raw, gain):
    unit, inverse = unit_of(raw)
    grad_normed = total * SCALE
    scaled = grad_normed * gain
    grad_raw = inverse * (scaled - unit * jnp.mean(scaled * unit, axis=-1, keepdims=True))
    return grad_raw.astype(bf16), jnp.sum(grad_normed * unit, axis=0, keepdims=True)


def last_kernel(
    copies,
    qx_ref, do_ref, kn_ref, v_ref, far_qx_ref, far_do_ref, far_kn_ref, far_v_ref, bias_ref,
    dq_in, dk_in, dv_in, query_ref, key_ref, qgain_ref, kgain_ref,
    query_grad_ref, key_grad_ref, value_grad_ref, terms_ref,
):
    offset = STEPS - 1

    def one_head(h, terms):
        lanes = head_lanes(h)
        _, grad_scores = pair_core(
            qx_ref, do_ref, far_kn_ref, far_v_ref, bias_ref, offset * ROUTE_MOST, lanes
        )
        total = dq_in[:, lanes] + dot_tn(grad_scores, far_kn_ref[:, lanes])
        query_grad_ref[:, lanes], query_term = norm_back(total, query_ref[:, lanes], qgain_ref[...])
        weights, grad_scores = pair_core(
            far_qx_ref, far_do_ref, kn_ref, v_ref, bias_ref, (STEPS - 1 + offset) * ROUTE_MOST, lanes
        )
        total = dk_in[:, lanes] + dot_nn(grad_scores, far_qx_ref[:CAP, lanes])
        key_grad_ref[:, lanes], key_term = norm_back(total, key_ref[:, lanes], kgain_ref[...])
        total = dv_in[:, lanes] + dot_nn(weights, far_do_ref[:, lanes])
        value_grad_ref[:, lanes] = total.astype(bf16)
        return terms[0] + query_term, terms[1] + key_term

    none = jnp.zeros((1, WIDTH), f32)
    query_term, key_term = lax.fori_loop(0, HEADS, one_head, (none, none), unroll=2)
    both = jnp.concatenate([query_term, key_term], axis=0)
    terms_ref[...] = jnp.broadcast_to(both[None], (copies, 2, WIDTH))


def sum_kernel(divisor, parts_ref, out_ref):
    total = jnp.sum(parts_ref[...], axis=0)
    out_ref[...] = jnp.broadcast_to((total / divisor)[None], out_ref.shape)


VMEM = pl.BlockSpec(memory_space=pltpu.VMEM)
SMEM = pl.BlockSpec(memory_space=pltpu.SMEM)


def call(kernel, outs, specs, flops, **options):
    return pl.pallas_call(
        kernel,
        out_shape=outs,
        in_specs=specs,
        out_specs=jax.tree.map(lambda _: VMEM, outs),
        cost_estimate=pl.CostEstimate(flops=flops, bytes_accessed=1 << 20, transcendentals=0),
        compiler_params=pltpu.CompilerParams(vmem_limit_bytes=32 << 20),
        **options,
    )


def passed_along(value, steps):
    count = lax.axis_size("tm")
    pairs = [(source, (source + steps) % count) for source in range(count)]
    return lax.ppermute(value, "tm", pairs)


def body(
    query_raw, key_raw, value_rows, grad_output, log_normalizer, output_dot,
    query_gain, key_gain, route_blocks, route_count, query_reach,
):
    shards, clips = lax.axis_size("tm"), lax.axis_size("dp")
    query, key, value, grad = query_raw[0], key_raw[0], value_rows[0], grad_output[0]
    qgain, kgain = query_gain[None], key_gain[None]

    def like(rows, dtype):
        return jax.ShapeDtypeStruct((rows, HD), dtype)

    far_v, far_do = passed_along(value, 1), passed_along(grad, -1)
    qx, kn, bias = call(
        prep_kernel,
        (like(CAP + STAT_ROWS, bf16), like(CAP, bf16), jax.ShapeDtypeStruct((16, CAP), f32)),
        [SMEM] * 3 + [VMEM] * 6,
        1 << 20,
    )(route_blocks, route_count, query_reach, query, key, log_normalizer[0], output_dot[0], qgain, kgain)
    far_kn, far_qx = passed_along(kn, 1), passed_along(qx, -1)
    totals = (like(CAP, f32),) * 3
    dq, dk, dv = call(own_kernel, totals, [VMEM] * 5, 1 << 30)(qx, grad, kn, value, bias)
    for offset in range(1, STEPS):
        now = (far_qx, far_do, far_kn, far_v)
        if offset < STEPS - 1:
            far_v, far_do = passed_along(far_v, 1), passed_along(far_do, -1)
            far_kn, far_qx = passed_along(far_kn, 1), passed_along(far_qx, -1)
            dq, dk, dv = call(
                functools.partial(step_kernel, offset),
                totals,
                [VMEM] * 12,
                1 << 30,
                input_output_aliases={9: 0, 10: 1, 11: 2},
            )(qx, grad, kn, value, *now, bias, dq, dk, dv)
    query_grad, key_grad, value_grad, terms = call(
        functools.partial(last_kernel, shards),
        (like(CAP, bf16),) * 3 + (jax.ShapeDtypeStruct((shards, 2, WIDTH), f32),),
        [VMEM] * 16,
        1 << 30,
    )(qx, grad, kn, value, *now, bias, dq, dk, dv, query, key, qgain, kgain)
    parts = lax.all_to_all(terms, "tm", 0, 0)
    sums = call(
        functools.partial(sum_kernel, 1.0),
        jax.ShapeDtypeStruct((clips, 2, WIDTH), f32),
        [VMEM],
        1 << 10,
    )(parts)
    parts = lax.all_to_all(sums, "dp", 0, 0)
    sums = jnp.sum(parts, axis=0) / (shards * clips)
    return (query_grad[None], key_grad[None], value_grad[None], sums[0], sums[1])


def solution(mesh):
    rows = P("dp", "tm", None)
    stats = P("dp", None, "tm")
    return jax.shard_map(
        body,
        mesh=mesh,
        in_specs=(
            rows, rows, rows, rows, stats, stats, P(), P(),
            P("dp", None, None), P("dp", None), P("dp", None),
        ),
        out_specs=(rows, rows, rows, P(), P()),
        check_vma=False,
    )
```

```python
import functools

import jax
import jax.numpy as jnp
from jax import lax
from jax.experimental import pallas as pl
from jax.experimental.pallas import tpu as pltpu
from jax.sharding import PartitionSpec as P

BLK = 64
NBLK = 3
ROUTE_MOST = 2
STEPS = 4
HEADS = 12
WIDTH = 128
CAP = ROUTE_MOST * BLK
HD = HEADS * WIDTH
STAT_ROWS = 16
ROWS = 2 * CAP + STAT_ROWS
FIRST, SECOND, STATS = slice(0, CAP), slice(CAP, 2 * CAP), slice(2 * CAP, ROWS)
LOG2E = 1.4426950408889634
SCALE = WIDTH**-0.5
CLOSED = -1e30
norm_eps = 1e-06

f32 = jnp.float32
bf16 = jnp.bfloat16


def head_lanes(h):
    return pl.ds(pl.multiple_of(h * WIDTH, WIDTH), WIDTH)


def over_heads(step, unroll=3):
    lax.fori_loop(0, HEADS, lambda h, none: step(h), None, unroll=unroll)


def by_parity(run, *chains):
    odd = lax.rem(lax.axis_index("tm"), 2)
    for parity in range(2):
        refs = []
        for a, b, hop in chains:
            refs += [a, b] if (parity + hop) % 2 == 0 else [b, a]

        @pl.when(odd == parity)
        def _():
            run(*refs)


def unit_of(raw):
    widened = raw.astype(f32)
    inverse = lax.rsqrt(jnp.mean(widened * widened, axis=-1, keepdims=True) + norm_eps)
    return widened * inverse, inverse


def three_parts(row):
    high = row.astype(bf16)
    rest = row - high.astype(f32)
    middle = rest.astype(bf16)
    low = (rest - middle.astype(f32)).astype(bf16)
    return high, middle, low


def prep_kernel(
    query_hbm, key_hbm, value_hbm, grad_hbm, log_hbm, dot_hbm, qgain_hbm, kgain_hbm,
    a_ref, b_ref,
    *scratch,
):
    by_parity(
        lambda up_ref, down_ref: prepare(
            query_hbm, key_hbm, value_hbm, grad_hbm, log_hbm, dot_hbm, qgain_hbm, kgain_hbm,
            up_ref, down_ref,
            *scratch,
        ),
        (a_ref, b_ref, 0),
    )


def prepare(
    query_hbm, key_hbm, value_hbm, grad_hbm, log_hbm, dot_hbm, qgain_hbm, kgain_hbm,
    up_ref, down_ref,
    query_ref, key_ref, log_ref, dot_ref, qgain_ref, kgain_ref, sems,
):
    moves = [
        pltpu.make_async_copy(source, target, sems.at[i])
        for i, (source, target) in enumerate(
            [
                (query_hbm.at[0], query_ref),
                (log_hbm, log_ref),
                (dot_hbm, dot_ref),
                (qgain_hbm, qgain_ref),
                (kgain_hbm, kgain_ref),
                (key_hbm.at[0], key_ref),
                (grad_hbm.at[0], down_ref.at[SECOND]),
                (value_hbm.at[0], up_ref.at[SECOND]),
            ]
        )
    ]
    for move in moves:
        move.start()
    for move in moves[:6]:
        move.wait()

    def one_head(h):
        lanes = head_lanes(h)
        unit, _ = unit_of(query_ref[:, lanes])
        down_ref[FIRST, lanes] = (unit * qgain_ref[...]).astype(bf16)
        unit, _ = unit_of(key_ref[:, lanes])
        up_ref[FIRST, lanes] = (unit * kgain_ref[...]).astype(bf16)
        parts = [
            p.astype(f32) for p in three_parts(log_ref[h] * -LOG2E) + three_parts(dot_ref[h])
        ]
        parts.append(jnp.zeros((STAT_ROWS - len(parts), CAP), f32))
        down_ref[STATS, lanes] = jnp.concatenate(parts, axis=0).astype(bf16)
        up_ref[STATS, lanes] = jnp.zeros((STAT_ROWS, CAP), bf16)

    over_heads(one_head)
    for move in moves[6:]:
        move.wait()


def stat_rows(down_ref, lanes):
    stats = down_ref[STATS, lanes].astype(f32)
    return stats[0:1] + stats[1:2] + stats[2:3], stats[3:4] + stats[4:5] + stats[5:6]


def dot_nt(a, b):
    return lax.dot_general(a, b, (((1,), (1,)), ((), ())), preferred_element_type=f32)


def dot_nn(a, b):
    return lax.dot_general(a, b, (((1,), (0,)), ((), ())), preferred_element_type=f32)


def dot_tn(a, b):
    return lax.dot_general(a, b, (((0,), (0,)), ((), ())), preferred_element_type=f32)


def side_by_side(parts, axis):
    return parts[0] if len(parts) == 1 else jnp.concatenate(parts, axis=axis)


def pair_core(up_ref, downs, lanes):
    logs, dots = zip(*(stat_rows(ref, lanes) for ref, _ in downs))
    queries = side_by_side([ref[FIRST, lanes] for ref, _ in downs], 0)
    cotangents = side_by_side([ref[SECOND, lanes] for ref, _ in downs], 0)
    scores = dot_nt(up_ref[FIRST, lanes], queries)
    half = []
    for j in range(ROUTE_MOST):
        row = side_by_side([log + bias[j : j + 1] for log, (_, bias) in zip(logs, downs)], 1)
        half.append(jnp.exp2(scores[j * BLK : (j + 1) * BLK] * (SCALE * LOG2E) + row))
    probability = jnp.concatenate(half, axis=0)
    grad_weights = dot_nt(up_ref[SECOND, lanes], cotangents)
    grad_scores = (probability * (grad_weights - side_by_side(dots, 1))).astype(bf16)
    return probability.astype(bf16), grad_scores, queries, cotangents


def rows_for_query(bias_ref, offset):
    return bias_ref[offset * ROUTE_MOST : (offset + 1) * ROUTE_MOST, :]


def rows_for_key(bias_ref, offset):
    return rows_for_query(bias_ref, STEPS - 1 + offset)


def rows_between(bias_ref):
    return rows_for_query(bias_ref, 2 * STEPS - 1)


def fill_bias(blocks_ref, counts_ref, reach_ref, bias_ref):
    shards = counts_ref.shape[1]
    here = lax.axis_index("tm")
    lane = lax.broadcasted_iota(jnp.int32, (1, CAP), 1)

    def pair_rows(query_shard, key_shard, offset):
        rows = []
        for kj in range(ROUTE_MOST):
            values = []
            for qi in range(ROUTE_MOST):
                near = (
                    offset * NBLK
                    + blocks_ref[0, qi, query_shard]
                    - blocks_ref[0, kj, key_shard]
                    < reach_ref[0, query_shard * ROUTE_MOST + qi]
                )
                live = (qi < counts_ref[0, query_shard]) & (kj < counts_ref[0, key_shard])
                values.append(jnp.where(near & live, 0.0, CLOSED).astype(f32))
            rows.append(jnp.where(lane < BLK, values[0], values[1]))
        return rows

    rows = []
    for offset in range(STEPS):
        rows += pair_rows(here, lax.rem(here - offset + shards, shards), offset)
    for offset in range(1, STEPS):
        rows += pair_rows(lax.rem(here + offset, shards), here, offset)
    rows += pair_rows(lax.rem(here + 1, shards), lax.rem(here - 2 + shards, shards), STEPS - 1)
    for at, row in enumerate(rows):
        bias_ref[at : at + 1, :] = row


def own_kernel(
    blocks_ref, counts_ref, reach_ref, a_ref, b_ref, query_ref, key_ref,
    dq_ref, dk_ref, dv_ref, bias_ref, query_unit_ref, query_inverse_ref, key_unit_ref, key_inverse_ref,
):
    fill_bias(blocks_ref, counts_ref, reach_ref, bias_ref)

    def run(up_ref, down_ref):
        def one_head(h):
            lanes = head_lanes(h)
            weights, grad_scores, queries, cotangents = pair_core(
                up_ref, [(down_ref, rows_for_query(bias_ref, 0))], lanes
            )
            dq_ref[:, lanes] = dot_tn(grad_scores, up_ref[FIRST, lanes])
            dk_ref[:, lanes] = dot_nn(grad_scores, queries)
            dv_ref[:, lanes] = dot_nn(weights, cotangents)
            for raw_ref, unit_ref, inverse_ref in (
                (query_ref, query_unit_ref, query_inverse_ref),
                (key_ref, key_unit_ref, key_inverse_ref),
            ):
                unit, inverse = unit_of(raw_ref[0, :, lanes])
                unit_ref[:, lanes] = unit
                inverse_ref[:, lanes] = jnp.broadcast_to(inverse, unit.shape)

        over_heads(one_head)

    by_parity(run, (a_ref, b_ref, 0))


def step_kernel(
    a_ref, b_ref, a1_ref, b1_ref, bias_ref, dq_in, dk_in, dv_in, dq_ref, dk_ref, dv_ref, token_ref
):
    def run(up_ref, down_ref, up1_ref, down1_ref):
        def one_head(h):
            lanes = head_lanes(h)
            _, grad_scores, _, _ = pair_core(
                up1_ref, [(down_ref, rows_for_query(bias_ref, 1))], lanes
            )
            dq_ref[:, lanes] = dq_in[:, lanes] + dot_tn(grad_scores, up1_ref[FIRST, lanes])
            weights, grad_scores, queries, cotangents = pair_core(
                up_ref, [(down1_ref, rows_for_key(bias_ref, 1))], lanes
            )
            dk_ref[:, lanes] = dk_in[:, lanes] + dot_nn(grad_scores, queries)
            dv_ref[:, lanes] = dv_in[:, lanes] + dot_nn(weights, cotangents)

        over_heads(one_head)

    by_parity(run, (a_ref, b_ref, 0), (a1_ref, b1_ref, 1))
    token_ref[...] = jnp.zeros(token_ref.shape, f32)


def terms_kernel(
    copies, a_ref, b_ref, a1_ref, b1_ref, a2_ref, b2_ref, bias_ref, dq_in, dk_ref,
    query_unit_ref, key_unit_ref, qgain_ref, kgain_ref, dq_ref, terms_ref,
):
    def run(up_ref, down_ref, up1_ref, down1_ref, up2_ref, down2_ref):
        def one_head(h, sums):
            lanes = head_lanes(h)
            _, grad_scores, queries, _ = pair_core(
                up2_ref,
                [(down_ref, rows_for_query(bias_ref, 2)), (down1_ref, rows_between(bias_ref))],
                lanes,
            )
            parts = dot_tn(grad_scores, up2_ref[FIRST, lanes])
            total = dq_in[:, lanes] + parts[:CAP]
            dq_ref[:, lanes] = total
            products = parts * queries.astype(f32)
            return (
                sums[0] + jnp.sum(total * query_unit_ref[:, lanes], axis=0, keepdims=True),
                sums[1]
                + jnp.sum(dk_ref[:, lanes] * key_unit_ref[:, lanes], axis=0, keepdims=True),
                sums[2] + jnp.sum(products[:CAP], axis=0, keepdims=True),
                sums[3] + jnp.sum(products[CAP:], axis=0, keepdims=True),
            )

        none = jnp.zeros((1, WIDTH), f32)
        for_query, for_key, two, three = lax.fori_loop(0, HEADS, one_head, (none,) * 4, unroll=3)
        for_query = for_query + three / qgain_ref[...]
        for_key = for_key + (two + three) / kgain_ref[...]
        both = jnp.concatenate([for_query, for_key], axis=0) * SCALE
        terms_ref[...] = jnp.broadcast_to(both[None], (copies, 2, WIDTH))

    by_parity(run, (a_ref, b_ref, 0), (a1_ref, b1_ref, 1), (a2_ref, b2_ref, 2))


def norm_back(total, unit, inverse, gain):
    scaled = total * (gain * SCALE)
    return (inverse * (scaled - unit * jnp.mean(scaled * unit, axis=-1, keepdims=True))).astype(bf16)


def last_kernel(
    divisor, a_ref, b_ref, a2_ref, b2_ref, a3_ref, b3_ref, bias_ref, dq_in, dk_in, dv_in,
    query_unit_ref, query_inverse_ref, key_unit_ref, key_inverse_ref, qgain_ref, kgain_ref, parts_ref,
    query_grad_ref, key_grad_ref, value_grad_ref, gains_ref,
):
    gains_ref[...] = jnp.sum(parts_ref[...], axis=0) / divisor

    def run(up_ref, down_ref, up2_ref, down2_ref, up3_ref, down3_ref):
        def one_head(h):
            lanes = head_lanes(h)
            _, grad_scores, _, _ = pair_core(
                up3_ref, [(down_ref, rows_for_query(bias_ref, 3))], lanes
            )
            total = dq_in[:, lanes] + dot_tn(grad_scores, up3_ref[FIRST, lanes])
            query_grad_ref[0, :, lanes] = norm_back(
                total, query_unit_ref[:, lanes], query_inverse_ref[:, lanes], qgain_ref[...]
            )
            weights, grad_scores, queries, cotangents = pair_core(
                up_ref,
                [(down2_ref, rows_for_key(bias_ref, 2)), (down3_ref, rows_for_key(bias_ref, 3))],
                lanes,
            )
            total = dk_in[:, lanes] + dot_nn(grad_scores, queries)
            key_grad_ref[0, :, lanes] = norm_back(
                total, key_unit_ref[:, lanes], key_inverse_ref[:, lanes], kgain_ref[...]
            )
            total = dv_in[:, lanes] + dot_nn(weights, cotangents)
            value_grad_ref[0, :, lanes] = total.astype(bf16)

        over_heads(one_head, 2)

    by_parity(run, (a_ref, b_ref, 0), (a2_ref, b2_ref, 2), (a3_ref, b3_ref, 3))


def sum_kernel(parts_ref, out_ref):
    total = jnp.sum(parts_ref[...], axis=0)
    out_ref[...] = jnp.broadcast_to(total[None], out_ref.shape)


def tie_kernel(chain_ref, token_ref, out_ref):
    pass


VMEM = pl.BlockSpec(memory_space=pltpu.VMEM)
SMEM = pl.BlockSpec(memory_space=pltpu.SMEM)
ANY = pl.BlockSpec(memory_space=pl.ANY)
HBM = pl.BlockSpec(memory_space=pltpu.HBM)


def call(kernel, outs, specs, operands, aliases=None, scratch=(), limit=16 << 20):
    return pl.pallas_call(
        kernel,
        out_shape=tuple(outs),
        in_specs=specs,
        out_specs=(VMEM,) * len(outs),
        scratch_shapes=list(scratch),
        input_output_aliases=aliases or {},
        cost_estimate=pl.CostEstimate(flops=1 << 29, bytes_accessed=1 << 20, transcendentals=0),
        compiler_params=pltpu.CompilerParams(vmem_limit_bytes=limit),
    )(*operands)


def after(chain, token):
    return pl.pallas_call(
        tie_kernel,
        out_shape=jax.ShapeDtypeStruct(chain.shape, chain.dtype),
        in_specs=[ANY, ANY],
        out_specs=ANY,
        input_output_aliases={0: 0},
        compiler_params=pltpu.CompilerParams(vmem_limit_bytes=1 << 20),
    )(chain, token)


def swapped(value, odd):
    count = lax.axis_size("tm")
    pairs = [(i, (i + 1 if i % 2 == odd else i - 1) % count) for i in range(count)]
    return lax.ppermute(value, "tm", pairs)


def body(
    query_raw, key_raw, value_rows, grad_output, log_normalizer, output_dot,
    query_gain, key_gain, route_blocks, route_count, query_reach,
):
    shards, clips = lax.axis_size("tm"), lax.axis_size("dp")
    qgain, kgain = query_gain[None], key_gain[None]

    def like(rows, dtype):
        return jax.ShapeDtypeStruct((rows, HD), dtype)

    total, wide = like(CAP, f32), like(ROWS, bf16)
    lines = jax.ShapeDtypeStruct((16, CAP), f32)
    a, b = call(
        prep_kernel,
        (wide, wide),
        [HBM] * 8,
        (
            query_raw, key_raw, value_rows, grad_output,
            jnp.swapaxes(log_normalizer, 0, 1), jnp.swapaxes(output_dot, 0, 1), qgain, kgain,
        ),
        scratch=(
            pltpu.VMEM((CAP, HD), bf16), pltpu.VMEM((CAP, HD), bf16),
            pltpu.VMEM((HEADS, 1, CAP), f32), pltpu.VMEM((HEADS, 1, CAP), f32),
            pltpu.VMEM((1, WIDTH), f32), pltpu.VMEM((1, WIDTH), f32),
            pltpu.SemaphoreType.DMA((8,)),
        ),
        limit=62 << 20,
    )
    a1, b1 = swapped(a, 0), swapped(b, 1)
    dq, dk, dv, bias, *units = call(
        own_kernel,
        (total, total, total, lines) + (total,) * 4,
        [SMEM] * 3 + [VMEM] * 4,
        (jnp.swapaxes(route_blocks, 1, 2), route_count, query_reach, a, b, query_raw, key_raw),
    )
    a1 = after(a1, bias)
    a2, b2 = swapped(a1, 1), swapped(b1, 0)
    dq, dk, dv, token = call(
        step_kernel,
        (total, total, total, lines),
        [VMEM] * 8,
        (a, b, a1, b1, bias, dq, dk, dv),
        {5: 0, 6: 1, 7: 2},
    )
    a2 = after(a2, token)
    a3, b3 = swapped(a2, 0), swapped(b2, 1)
    dq, terms = call(
        functools.partial(terms_kernel, clips),
        (total, jax.ShapeDtypeStruct((clips, 2, WIDTH), f32)),
        [VMEM] * 13,
        (a, b, a1, b1, a2, b2, bias, dq, dk, units[0], units[2], qgain, kgain),
        {7: 0},
    )
    parts = lax.all_to_all(terms, "dp", 0, 0)
    (sums,) = call(
        sum_kernel, (jax.ShapeDtypeStruct((shards, 2, WIDTH), f32),), [VMEM], (parts,)
    )
    parts = lax.all_to_all(sums, "tm", 0, 0)
    row = jax.ShapeDtypeStruct((1, CAP, HD), bf16)
    query_grad, key_grad, value_grad, gains = call(
        functools.partial(last_kernel, shards * clips),
        (row, row, row, jax.ShapeDtypeStruct((2, WIDTH), f32)),
        [VMEM] * 17,
        (a, b, a2, b2, a3, b3, bias, dq, dk, dv, *units, qgain, kgain, parts),
    )
    return (query_grad, key_grad, value_grad, gains[0], gains[1])


def solution(mesh):
    rows = P("dp", "tm", None)
    stats = P("dp", None, "tm")
    return jax.shard_map(
        body,
        mesh=mesh,
        in_specs=(
            rows, rows, rows, rows, stats, stats, P(), P(),
            P("dp", None, None), P("dp", None), P("dp", None),
        ),
        out_specs=(rows, rows, rows, P(), P()),
        check_vma=False,
    )
```

```python
import functools

import jax
import jax.numpy as jnp
from jax import lax
from jax.experimental import pallas as pl
from jax.experimental.pallas import tpu as pltpu
from jax.sharding import PartitionSpec as P

BLK = 64
NBLK = 3
ROUTE_MOST = 2
STEPS = 4
HEADS = 12
WIDTH = 128
CAP = ROUTE_MOST * BLK
HD = HEADS * WIDTH
STAT_ROWS = 8
ROWS = 2 * CAP + STAT_ROWS
FIRST, SECOND, STATS = slice(0, CAP), slice(CAP, 2 * CAP), slice(2 * CAP, ROWS)
LOG2E = 1.4426950408889634
SCALE = WIDTH**-0.5
CLOSED = -1e30
norm_eps = 1e-06

f32 = jnp.float32
bf16 = jnp.bfloat16


def head_lanes(h):
    return pl.ds(pl.multiple_of(h * WIDTH, WIDTH), WIDTH)


def over_heads(step, unroll=HEADS):
    lax.fori_loop(0, HEADS, lambda h, none: step(h), None, unroll=unroll)


def by_parity(run, *chains):
    odd = lax.rem(lax.axis_index("tm"), 2)
    for parity in range(2):
        refs = []
        for a, b, hop in chains:
            refs += [a, b] if (parity + hop) % 2 == 0 else [b, a]

        @pl.when(odd == parity)
        def _():
            run(*refs)


def unit_of(raw):
    widened = raw.astype(f32)
    inverse = lax.rsqrt(jnp.mean(widened * widened, axis=-1, keepdims=True) + norm_eps)
    return widened * inverse, inverse


def three_parts(row):
    high = row.astype(bf16)
    rest = row - high.astype(f32)
    middle = rest.astype(bf16)
    low = (rest - middle.astype(f32)).astype(bf16)
    return high, middle, low


def prep_kernel(
    query_hbm, key_hbm, value_hbm, grad_hbm, log_hbm, dot_hbm, qgain_hbm, kgain_hbm,
    a_ref, b_ref,
    *scratch,
):
    by_parity(
        lambda up_ref, down_ref: prepare(
            query_hbm, key_hbm, value_hbm, grad_hbm, log_hbm, dot_hbm, qgain_hbm, kgain_hbm,
            up_ref, down_ref,
            *scratch,
        ),
        (a_ref, b_ref, 0),
    )


def prepare(
    query_hbm, key_hbm, value_hbm, grad_hbm, log_hbm, dot_hbm, qgain_hbm, kgain_hbm,
    up_ref, down_ref,
    query_ref, key_ref, log_ref, dot_ref, qgain_ref, kgain_ref, sems,
):
    moves = [
        pltpu.make_async_copy(source, target, sems.at[i])
        for i, (source, target) in enumerate(
            [
                (query_hbm.at[0], query_ref),
                (log_hbm, log_ref),
                (dot_hbm, dot_ref),
                (qgain_hbm, qgain_ref),
                (kgain_hbm, kgain_ref),
                (key_hbm.at[0], key_ref),
                (grad_hbm.at[0], down_ref.at[SECOND]),
                (value_hbm.at[0], up_ref.at[SECOND]),
            ]
        )
    ]
    for move in moves:
        move.start()
    for move in moves[:6]:
        move.wait()

    def one_head(h):
        lanes = head_lanes(h)
        unit, _ = unit_of(query_ref[:, lanes])
        down_ref[FIRST, lanes] = (unit * qgain_ref[...]).astype(bf16)
        unit, _ = unit_of(key_ref[:, lanes])
        up_ref[FIRST, lanes] = (unit * kgain_ref[...]).astype(bf16)
        parts = [
            p.astype(f32) for p in three_parts(log_ref[h] * -LOG2E) + three_parts(dot_ref[h])
        ]
        parts.append(jnp.zeros((STAT_ROWS - len(parts), CAP), f32))
        down_ref[STATS, lanes] = jnp.concatenate(parts, axis=0).astype(bf16)
        up_ref[STATS, lanes] = jnp.zeros((STAT_ROWS, CAP), bf16)

    over_heads(one_head)
    for move in moves[6:]:
        move.wait()


def stat_rows(down_ref, lanes):
    stats = down_ref[STATS, lanes].astype(f32)
    return stats[0:1] + stats[1:2] + stats[2:3], stats[3:4] + stats[4:5] + stats[5:6]


def dot_nt(a, b):
    return lax.dot_general(a, b, (((1,), (1,)), ((), ())), preferred_element_type=f32)


def dot_nn(a, b):
    return lax.dot_general(a, b, (((1,), (0,)), ((), ())), preferred_element_type=f32)


def dot_tn(a, b):
    return lax.dot_general(a, b, (((0,), (0,)), ((), ())), preferred_element_type=f32)


def side_by_side(parts, axis):
    return parts[0] if len(parts) == 1 else jnp.concatenate(parts, axis=axis)


def pair_core(up_ref, downs, lanes):
    logs, dots = zip(*(stat_rows(ref, lanes) for ref, _ in downs))
    queries = side_by_side([ref[FIRST, lanes] for ref, _ in downs], 0)
    cotangents = side_by_side([ref[SECOND, lanes] for ref, _ in downs], 0)
    scores = dot_nt(up_ref[FIRST, lanes], queries)
    half = []
    for j in range(ROUTE_MOST):
        row = side_by_side([log + bias[j : j + 1] for log, (_, bias) in zip(logs, downs)], 1)
        half.append(jnp.exp2(scores[j * BLK : (j + 1) * BLK] * (SCALE * LOG2E) + row))
    probability = jnp.concatenate(half, axis=0)
    grad_weights = dot_nt(up_ref[SECOND, lanes], cotangents)
    grad_scores = (probability * (grad_weights - side_by_side(dots, 1))).astype(bf16)
    return probability.astype(bf16), grad_scores, queries, cotangents


def rows_for_query(bias_ref, offset):
    return bias_ref[offset * ROUTE_MOST : (offset + 1) * ROUTE_MOST, :]


def rows_for_key(bias_ref, offset):
    return rows_for_query(bias_ref, STEPS - 1 + offset)


def by_query(bias_ref, which):
    at = (2 * STEPS - 1 + which) * ROUTE_MOST
    return bias_ref[at : at + ROUTE_MOST, :]


def as_column(row):
    return jnp.transpose(jnp.broadcast_to(row, (CAP, CAP)))


def with_bias(column, bias):
    return jnp.concatenate(
        [column[i * BLK : (i + 1) * BLK] + bias[i : i + 1] for i in range(ROUTE_MOST)], axis=0
    )


def grad_query_core(up_ref, downs, lanes):
    queries = side_by_side([ref[FIRST, lanes] for ref, _, _ in downs], 0)
    cotangents = side_by_side([ref[SECOND, lanes] for ref, _, _ in downs], 0)
    known = side_by_side([ref[:, lanes] for _, ref, _ in downs], 0)
    dots = side_by_side([ref[:, lanes] for _, _, ref in downs], 0)
    probability = jnp.exp2(dot_nt(queries, up_ref[FIRST, lanes]) * (SCALE * LOG2E) + known)
    grad_weights = dot_nt(cotangents, up_ref[SECOND, lanes])
    grad_scores = (probability * (grad_weights - dots)).astype(bf16)
    return dot_nn(grad_scores, up_ref[FIRST, lanes]), queries


def fill_bias(blocks_ref, counts_ref, reach_ref, bias_ref):
    shards = counts_ref.shape[1]
    here = lax.axis_index("tm")
    lane = lax.broadcasted_iota(jnp.int32, (1, CAP), 1)

    def pair_rows(query_shard, key_shard, offset, by_query=False):
        rows = []
        for outer in range(ROUTE_MOST):
            values = []
            for inner in range(ROUTE_MOST):
                qi, kj = (outer, inner) if by_query else (inner, outer)
                near = (
                    offset * NBLK
                    + blocks_ref[0, qi, query_shard]
                    - blocks_ref[0, kj, key_shard]
                    < reach_ref[0, query_shard * ROUTE_MOST + qi]
                )
                live = (qi < counts_ref[0, query_shard]) & (kj < counts_ref[0, key_shard])
                values.append(jnp.where(near & live, 0.0, CLOSED).astype(f32))
            rows.append(jnp.where(lane < BLK, values[0], values[1]))
        return rows

    rows = []
    for offset in range(STEPS):
        rows += pair_rows(here, lax.rem(here - offset + shards, shards), offset)
    for offset in range(1, STEPS):
        rows += pair_rows(lax.rem(here + offset, shards), here, offset)
    two_back = lax.rem(here - 2 + shards, shards)
    rows += pair_rows(here, two_back, 2, True)
    rows += pair_rows(here, lax.rem(here - 3 + shards, shards), 3, True)
    rows += pair_rows(lax.rem(here + 1, shards), two_back, 3, True)
    rows += [jnp.zeros((1, CAP), f32)] * (bias_ref.shape[0] - len(rows))
    for at, row in enumerate(rows):
        bias_ref[at : at + 1, :] = row


def own_kernel(
    blocks_ref, counts_ref, reach_ref, a_ref, b_ref, query_ref, key_ref,
    dq_ref, dk_ref, dv_ref, bias_ref, query_unit_ref, query_inverse_ref, key_unit_ref, key_inverse_ref,
    two_ref, three_ref, dot_ref,
):
    fill_bias(blocks_ref, counts_ref, reach_ref, bias_ref)

    def run(up_ref, down_ref):
        def one_head(h):
            lanes = head_lanes(h)
            weights, grad_scores, queries, cotangents = pair_core(
                up_ref, [(down_ref, rows_for_query(bias_ref, 0))], lanes
            )
            dq_ref[:, lanes] = dot_tn(grad_scores, up_ref[FIRST, lanes])
            dk_ref[:, lanes] = dot_nn(grad_scores, queries)
            dv_ref[:, lanes] = dot_nn(weights, cotangents)
            for raw_ref, unit_ref, inverse_ref in (
                (query_ref, query_unit_ref, query_inverse_ref),
                (key_ref, key_unit_ref, key_inverse_ref),
            ):
                unit, inverse = unit_of(raw_ref[0, :, lanes])
                unit_ref[:, lanes] = unit
                inverse_ref[:, lanes] = jnp.broadcast_to(inverse, unit.shape)
            log_row, dot_row = stat_rows(down_ref, lanes)
            column = as_column(log_row)
            two_ref[:, lanes] = with_bias(column, by_query(bias_ref, 0))
            three_ref[:, lanes] = with_bias(column, by_query(bias_ref, 1))
            dot_ref[:, lanes] = as_column(dot_row)

        over_heads(one_head)

    by_parity(run, (a_ref, b_ref, 0))


def step_kernel(
    a_ref, b_ref, a1_ref, b1_ref, bias_ref, dq_in, dk_in, dv_in, dq_ref, dk_ref, dv_ref, token_ref,
    next_three_ref, next_dot_ref,
):
    def run(up_ref, down_ref, up1_ref, down1_ref):
        def one_head(h):
            lanes = head_lanes(h)
            _, grad_scores, _, _ = pair_core(
                up1_ref, [(down_ref, rows_for_query(bias_ref, 1))], lanes
            )
            dq_ref[:, lanes] = dq_in[:, lanes] + dot_tn(grad_scores, up1_ref[FIRST, lanes])
            weights, grad_scores, queries, cotangents = pair_core(
                up_ref, [(down1_ref, rows_for_key(bias_ref, 1))], lanes
            )
            dk_ref[:, lanes] = dk_in[:, lanes] + dot_nn(grad_scores, queries)
            dv_ref[:, lanes] = dv_in[:, lanes] + dot_nn(weights, cotangents)
            log_row, dot_row = stat_rows(down1_ref, lanes)
            next_three_ref[:, lanes] = with_bias(as_column(log_row), by_query(bias_ref, 2))
            next_dot_ref[:, lanes] = as_column(dot_row)

        over_heads(one_head)

    by_parity(run, (a_ref, b_ref, 0), (a1_ref, b1_ref, 1))
    token_ref[...] = jnp.zeros(token_ref.shape, f32)


def terms_kernel(
    copies, a_ref, b_ref, a1_ref, b1_ref, a2_ref, b2_ref, dq_in, dk_ref,
    query_unit_ref, key_unit_ref, qgain_ref, kgain_ref, two_ref, dot_ref, next_three_ref, next_dot_ref,
    dq_ref, terms_ref,
):
    def run(up_ref, down_ref, up1_ref, down1_ref, up2_ref, down2_ref):
        def one_head(h, sums):
            lanes = head_lanes(h)
            parts, queries = grad_query_core(
                up2_ref,
                [(down_ref, two_ref, dot_ref), (down1_ref, next_three_ref, next_dot_ref)],
                lanes,
            )
            total = dq_in[:, lanes] + parts[:CAP]
            dq_ref[:, lanes] = total
            products = parts * queries.astype(f32)
            return (
                sums[0] + jnp.sum(total * query_unit_ref[:, lanes], axis=0, keepdims=True),
                sums[1]
                + jnp.sum(dk_ref[:, lanes] * key_unit_ref[:, lanes], axis=0, keepdims=True),
                sums[2] + jnp.sum(products[:CAP], axis=0, keepdims=True),
                sums[3] + jnp.sum(products[CAP:], axis=0, keepdims=True),
            )

        none = jnp.zeros((1, WIDTH), f32)
        for_query, for_key, two, three = lax.fori_loop(0, HEADS, one_head, (none,) * 4, unroll=HEADS)
        for_query = for_query + three / qgain_ref[...]
        for_key = for_key + (two + three) / kgain_ref[...]
        both = jnp.concatenate([for_query, for_key], axis=0) * SCALE
        terms_ref[...] = jnp.broadcast_to(both[None], (copies, 2, WIDTH))

    by_parity(run, (a_ref, b_ref, 0), (a1_ref, b1_ref, 1), (a2_ref, b2_ref, 2))


def norm_back(total, unit, inverse, gain):
    scaled = total * (gain * SCALE)
    return (inverse * (scaled - unit * jnp.mean(scaled * unit, axis=-1, keepdims=True))).astype(bf16)


def last_kernel(
    divisor, a_ref, b_ref, a2_ref, b2_ref, a3_ref, b3_ref, bias_ref, dq_in, dk_in, dv_in,
    query_unit_ref, query_inverse_ref, key_unit_ref, key_inverse_ref, qgain_ref, kgain_ref,
    three_ref, dot_ref, parts_ref,
    query_grad_ref, key_grad_ref, value_grad_ref, gains_ref,
):
    gains_ref[...] = jnp.sum(parts_ref[...], axis=0) / divisor

    def run(up_ref, down_ref, up2_ref, down2_ref, up3_ref, down3_ref):
        def one_head(h):
            lanes = head_lanes(h)
            part, _ = grad_query_core(up3_ref, [(down_ref, three_ref, dot_ref)], lanes)
            total = dq_in[:, lanes] + part
            query_grad_ref[0, :, lanes] = norm_back(
                total, query_unit_ref[:, lanes], query_inverse_ref[:, lanes], qgain_ref[...]
            )
            weights, grad_scores, queries, cotangents = pair_core(
                up_ref,
                [(down2_ref, rows_for_key(bias_ref, 2)), (down3_ref, rows_for_key(bias_ref, 3))],
                lanes,
            )
            total = dk_in[:, lanes] + dot_nn(grad_scores, queries)
            key_grad_ref[0, :, lanes] = norm_back(
                total, key_unit_ref[:, lanes], key_inverse_ref[:, lanes], kgain_ref[...]
            )
            total = dv_in[:, lanes] + dot_nn(weights, cotangents)
            value_grad_ref[0, :, lanes] = total.astype(bf16)

        over_heads(one_head)

    by_parity(run, (a_ref, b_ref, 0), (a2_ref, b2_ref, 2), (a3_ref, b3_ref, 3))


def sum_kernel(parts_ref, out_ref):
    total = jnp.sum(parts_ref[...], axis=0)
    out_ref[...] = jnp.broadcast_to(total[None], out_ref.shape)


def tie_kernel(chain_ref, token_ref, out_ref):
    pass


VMEM = pl.BlockSpec(memory_space=pltpu.VMEM)
SMEM = pl.BlockSpec(memory_space=pltpu.SMEM)
ANY = pl.BlockSpec(memory_space=pl.ANY)
HBM = pl.BlockSpec(memory_space=pltpu.HBM)


def call(kernel, outs, specs, operands, aliases=None, scratch=(), limit=16 << 20):
    return pl.pallas_call(
        kernel,
        out_shape=tuple(outs),
        in_specs=specs,
        out_specs=(VMEM,) * len(outs),
        scratch_shapes=list(scratch),
        input_output_aliases=aliases or {},
        cost_estimate=pl.CostEstimate(flops=1 << 29, bytes_accessed=1 << 20, transcendentals=0),
        compiler_params=pltpu.CompilerParams(vmem_limit_bytes=limit),
    )(*operands)


def after(chain, token):
    return pl.pallas_call(
        tie_kernel,
        out_shape=jax.ShapeDtypeStruct(chain.shape, chain.dtype),
        in_specs=[ANY, ANY],
        out_specs=ANY,
        input_output_aliases={0: 0},
        compiler_params=pltpu.CompilerParams(vmem_limit_bytes=1 << 20),
    )(chain, token)


def swapped(value, odd):
    count = lax.axis_size("tm")
    pairs = [(i, (i + 1 if i % 2 == odd else i - 1) % count) for i in range(count)]
    return lax.ppermute(value, "tm", pairs)


def body(
    query_raw, key_raw, value_rows, grad_output, log_normalizer, output_dot,
    query_gain, key_gain, route_blocks, route_count, query_reach,
):
    shards, clips = lax.axis_size("tm"), lax.axis_size("dp")
    qgain, kgain = query_gain[None], key_gain[None]

    def like(rows, dtype):
        return jax.ShapeDtypeStruct((rows, HD), dtype)

    total, wide = like(CAP, f32), like(ROWS, bf16)
    lines = jax.ShapeDtypeStruct((24, CAP), f32)
    a, b = call(
        prep_kernel,
        (wide, wide),
        [HBM] * 8,
        (
            query_raw, key_raw, value_rows, grad_output,
            jnp.swapaxes(log_normalizer, 0, 1), jnp.swapaxes(output_dot, 0, 1), qgain, kgain,
        ),
        scratch=(
            pltpu.VMEM((CAP, HD), bf16), pltpu.VMEM((CAP, HD), bf16),
            pltpu.VMEM((HEADS, 1, CAP), f32), pltpu.VMEM((HEADS, 1, CAP), f32),
            pltpu.VMEM((1, WIDTH), f32), pltpu.VMEM((1, WIDTH), f32),
            pltpu.SemaphoreType.DMA((8,)),
        ),
        limit=62 << 20,
    )
    a1, b1 = swapped(a, 0), swapped(b, 1)
    dq, dk, dv, bias, *units, two, three, dots = call(
        own_kernel,
        (total, total, total, lines) + (total,) * 7,
        [SMEM] * 3 + [VMEM] * 4,
        (jnp.swapaxes(route_blocks, 1, 2), route_count, query_reach, a, b, query_raw, key_raw),
    )
    a1 = after(a1, bias)
    a2, b2 = swapped(a1, 1), swapped(b1, 0)
    dq, dk, dv, token, next_three, next_dots = call(
        step_kernel,
        (total, total, total, lines, total, total),
        [VMEM] * 8,
        (a, b, a1, b1, bias, dq, dk, dv),
        {5: 0, 6: 1, 7: 2},
    )
    b2 = after(b2, token)
    b3, a3 = swapped(b2, 1), swapped(a2, 0)
    ends = 2 if clips % 4 == 0 else 1
    first = [
        [clip for clip in range(clips) if clip // 2 % ends == end] for end in range(ends)
    ]
    second = [
        [shard * clips + clip for shard in range(shards) for clip in column]
        for column in zip(*first)
    ]
    dq, terms = call(
        functools.partial(terms_kernel, len(first[0])),
        (total, jax.ShapeDtypeStruct((len(first[0]), 2, WIDTH), f32)),
        [VMEM] * 16,
        (
            a, b, a1, b1, a2, b2, dq, dk, units[0], units[2], qgain, kgain,
            two, dots, next_three, next_dots,
        ),
        {6: 0},
    )
    parts = lax.all_to_all(terms, "dp", 0, 0, axis_index_groups=first)
    (sums,) = call(
        sum_kernel, (jax.ShapeDtypeStruct((len(second[0]), 2, WIDTH), f32),), [VMEM], (parts,)
    )
    parts = lax.all_to_all(sums, ("tm", "dp"), 0, 0, axis_index_groups=second)
    row = jax.ShapeDtypeStruct((1, CAP, HD), bf16)
    query_grad, key_grad, value_grad, gains = call(
        functools.partial(last_kernel, shards * clips),
        (row, row, row, jax.ShapeDtypeStruct((2, WIDTH), f32)),
        [VMEM] * 19,
        (
            a, b, a2, b2, a3, b3, bias, dq, dk, dv, *units, qgain, kgain,
            three, dots, parts,
        ),
    )
    return (query_grad, key_grad, value_grad, gains[0], gains[1])


def solution(mesh):
    rows = P("dp", "tm", None)
    stats = P("dp", None, "tm")
    return jax.shard_map(
        body,
        mesh=mesh,
        in_specs=(
            rows, rows, rows, rows, stats, stats, P(), P(),
            P("dp", None, None), P("dp", None), P("dp", None),
        ),
        out_specs=(rows, rows, rows, P(), P()),
        check_vma=False,
    )
```

```python
import functools

import jax
import jax.numpy as jnp
from jax import lax
from jax.experimental import pallas as pl
from jax.experimental.pallas import tpu as pltpu
from jax.sharding import PartitionSpec as P

BLK = 64
NBLK = 3
ROUTE_MOST = 2
STEPS = 4
HEADS = 12
WIDTH = 128
CAP = ROUTE_MOST * BLK
HD = HEADS * WIDTH
STAT_ROWS = 8
ROWS = 2 * CAP + STAT_ROWS
FIRST, SECOND, STATS = slice(0, CAP), slice(CAP, 2 * CAP), slice(2 * CAP, ROWS)
LOG2E = 1.4426950408889634
SCALE = WIDTH**-0.5
CLOSED = -1e30
norm_eps = 1e-06
LAST_GROUPS = 3
LAST_LIMIT = 60 << 20

f32 = jnp.float32
bf16 = jnp.bfloat16


def head_lanes(h):
    return pl.ds(pl.multiple_of(h * WIDTH, WIDTH), WIDTH)


def over_heads(step, unroll=HEADS):
    lax.fori_loop(0, HEADS, lambda h, none: step(h), None, unroll=unroll)


def by_parity(run, *chains):
    odd = lax.rem(lax.axis_index("tm"), 2)
    for parity in range(2):
        refs = []
        for a, b, hop in chains:
            refs += [a, b] if (parity + hop) % 2 == 0 else [b, a]

        @pl.when(odd == parity)
        def _():
            run(*refs)


def unit_of(raw):
    widened = raw.astype(f32)
    inverse = lax.rsqrt(jnp.mean(widened * widened, axis=-1, keepdims=True) + norm_eps)
    return widened * inverse, inverse


def three_parts(row):
    high = row.astype(bf16)
    rest = row - high.astype(f32)
    middle = rest.astype(bf16)
    low = (rest - middle.astype(f32)).astype(bf16)
    return high, middle, low


def prep_kernel(
    query_hbm, key_hbm, value_hbm, grad_hbm, log_hbm, dot_hbm, qgain_hbm, kgain_hbm,
    a_ref, b_ref,
    *scratch,
):
    by_parity(
        lambda up_ref, down_ref: prepare(
            query_hbm, key_hbm, value_hbm, grad_hbm, log_hbm, dot_hbm, qgain_hbm, kgain_hbm,
            up_ref, down_ref,
            *scratch,
        ),
        (a_ref, b_ref, 0),
    )


def prepare(
    query_hbm, key_hbm, value_hbm, grad_hbm, log_hbm, dot_hbm, qgain_hbm, kgain_hbm,
    up_ref, down_ref,
    query_ref, key_ref, log_ref, dot_ref, qgain_ref, kgain_ref, sems,
):
    moves = [
        pltpu.make_async_copy(source, target, sems.at[i])
        for i, (source, target) in enumerate(
            [
                (query_hbm.at[0], query_ref),
                (log_hbm, log_ref),
                (dot_hbm, dot_ref),
                (qgain_hbm, qgain_ref),
                (kgain_hbm, kgain_ref),
                (key_hbm.at[0], key_ref),
                (grad_hbm.at[0], down_ref.at[SECOND]),
                (value_hbm.at[0], up_ref.at[SECOND]),
            ]
        )
    ]
    for move in moves:
        move.start()
    for move in moves[:6]:
        move.wait()

    def one_head(h):
        lanes = head_lanes(h)
        unit, _ = unit_of(query_ref[:, lanes])
        down_ref[FIRST, lanes] = (unit * qgain_ref[...]).astype(bf16)
        unit, _ = unit_of(key_ref[:, lanes])
        up_ref[FIRST, lanes] = (unit * kgain_ref[...]).astype(bf16)
        parts = [
            p.astype(f32) for p in three_parts(log_ref[h] * -LOG2E) + three_parts(dot_ref[h])
        ]
        parts.append(jnp.zeros((STAT_ROWS - len(parts), CAP), f32))
        down_ref[STATS, lanes] = jnp.concatenate(parts, axis=0).astype(bf16)
        up_ref[STATS, lanes] = jnp.zeros((STAT_ROWS, CAP), bf16)

    over_heads(one_head)
    for move in moves[6:]:
        move.wait()


def stat_rows(down_ref, lanes):
    stats = down_ref[STATS, lanes].astype(f32)
    return stats[0:1] + stats[1:2] + stats[2:3], stats[3:4] + stats[4:5] + stats[5:6]


def dot_nt(a, b):
    return lax.dot_general(a, b, (((1,), (1,)), ((), ())), preferred_element_type=f32)


def dot_nn(a, b):
    return lax.dot_general(a, b, (((1,), (0,)), ((), ())), preferred_element_type=f32)


def dot_tn(a, b):
    return lax.dot_general(a, b, (((0,), (0,)), ((), ())), preferred_element_type=f32)


def side_by_side(parts, axis):
    return parts[0] if len(parts) == 1 else jnp.concatenate(parts, axis=axis)


def pair_core(up_ref, downs, lanes):
    logs, dots = zip(*(stat_rows(ref, lanes) for ref, _ in downs))
    queries = side_by_side([ref[FIRST, lanes] for ref, _ in downs], 0)
    cotangents = side_by_side([ref[SECOND, lanes] for ref, _ in downs], 0)
    scores = dot_nt(up_ref[FIRST, lanes], queries)
    half = []
    for j in range(ROUTE_MOST):
        row = side_by_side([log + bias[j : j + 1] for log, (_, bias) in zip(logs, downs)], 1)
        half.append(jnp.exp2(scores[j * BLK : (j + 1) * BLK] * (SCALE * LOG2E) + row))
    probability = jnp.concatenate(half, axis=0)
    grad_weights = dot_nt(up_ref[SECOND, lanes], cotangents)
    grad_scores = (probability * (grad_weights - side_by_side(dots, 1))).astype(bf16)
    return probability.astype(bf16), grad_scores, queries, cotangents


def rows_for_query(bias_ref, offset):
    return bias_ref[offset * ROUTE_MOST : (offset + 1) * ROUTE_MOST, :]


def rows_for_key(bias_ref, offset):
    return rows_for_query(bias_ref, STEPS - 1 + offset)


def by_query(bias_ref, which):
    at = (2 * STEPS - 1 + which) * ROUTE_MOST
    return bias_ref[at : at + ROUTE_MOST, :]


def as_column(row):
    return jnp.transpose(jnp.broadcast_to(row, (CAP, CAP)))


def with_bias(column, bias):
    return jnp.concatenate(
        [column[i * BLK : (i + 1) * BLK] + bias[i : i + 1] for i in range(ROUTE_MOST)], axis=0
    )


def grad_query_core(up_ref, downs, lanes):
    queries = side_by_side([ref[FIRST, lanes] for ref, _, _ in downs], 0)
    cotangents = side_by_side([ref[SECOND, lanes] for ref, _, _ in downs], 0)
    known = side_by_side([ref[:, lanes] for _, ref, _ in downs], 0)
    dots = side_by_side([ref[:, lanes] for _, _, ref in downs], 0)
    probability = jnp.exp2(dot_nt(queries, up_ref[FIRST, lanes]) * (SCALE * LOG2E) + known)
    grad_weights = dot_nt(cotangents, up_ref[SECOND, lanes])
    grad_scores = (probability * (grad_weights - dots)).astype(bf16)
    return dot_nn(grad_scores, up_ref[FIRST, lanes]), queries


def fill_bias(blocks_ref, counts_ref, reach_ref, bias_ref):
    shards = counts_ref.shape[1]
    here = lax.axis_index("tm")
    lane = lax.broadcasted_iota(jnp.int32, (1, CAP), 1)

    def pair_rows(query_shard, key_shard, offset, by_query=False):
        rows = []
        for outer in range(ROUTE_MOST):
            values = []
            for inner in range(ROUTE_MOST):
                qi, kj = (outer, inner) if by_query else (inner, outer)
                near = (
                    offset * NBLK
                    + blocks_ref[0, qi, query_shard]
                    - blocks_ref[0, kj, key_shard]
                    < reach_ref[0, query_shard * ROUTE_MOST + qi]
                )
                live = (qi < counts_ref[0, query_shard]) & (kj < counts_ref[0, key_shard])
                values.append(jnp.where(near & live, 0.0, CLOSED).astype(f32))
            rows.append(jnp.where(lane < BLK, values[0], values[1]))
        return rows

    rows = []
    for offset in range(STEPS):
        rows += pair_rows(here, lax.rem(here - offset + shards, shards), offset)
    for offset in range(1, STEPS):
        rows += pair_rows(lax.rem(here + offset, shards), here, offset)
    two_back = lax.rem(here - 2 + shards, shards)
    rows += pair_rows(here, two_back, 2, True)
    rows += pair_rows(here, lax.rem(here - 3 + shards, shards), 3, True)
    rows += pair_rows(lax.rem(here + 1, shards), two_back, 3, True)
    rows += [jnp.zeros((1, CAP), f32)] * (bias_ref.shape[0] - len(rows))
    for at, row in enumerate(rows):
        bias_ref[at : at + 1, :] = row


def own_kernel(
    blocks_ref, counts_ref, reach_ref, a_ref, b_ref, query_ref, key_ref, qgain_ref, kgain_ref,
    dq_ref, dk_ref, dv_ref, bias_ref, query_unit_ref, query_inverse_ref, key_unit_ref, key_inverse_ref,
    two_ref, three_ref, dot_ref, gains_ref,
):
    fill_bias(blocks_ref, counts_ref, reach_ref, bias_ref)
    gains_ref[...] = jnp.concatenate([qgain_ref[...], kgain_ref[...]], axis=0)

    def run(up_ref, down_ref):
        def one_head(h):
            lanes = head_lanes(h)
            weights, grad_scores, queries, cotangents = pair_core(
                up_ref, [(down_ref, rows_for_query(bias_ref, 0))], lanes
            )
            dq_ref[:, lanes] = dot_tn(grad_scores, up_ref[FIRST, lanes])
            dk_ref[:, lanes] = dot_nn(grad_scores, queries)
            dv_ref[:, lanes] = dot_nn(weights, cotangents)
            for raw_ref, unit_ref, inverse_ref in (
                (query_ref, query_unit_ref, query_inverse_ref),
                (key_ref, key_unit_ref, key_inverse_ref),
            ):
                unit, inverse = unit_of(raw_ref[0, :, lanes])
                unit_ref[:, lanes] = unit
                inverse_ref[:, lanes] = jnp.broadcast_to(inverse, unit.shape)
            log_row, dot_row = stat_rows(down_ref, lanes)
            column = as_column(log_row)
            two_ref[:, lanes] = with_bias(column, by_query(bias_ref, 0))
            three_ref[:, lanes] = with_bias(column, by_query(bias_ref, 1))
            dot_ref[:, lanes] = as_column(dot_row)

        over_heads(one_head)

    by_parity(run, (a_ref, b_ref, 0))


def step_kernel(
    a_ref, b_ref, a1_ref, b1_ref, bias_ref, dq_in, dk_in, dv_in, dq_ref, dk_ref, dv_ref, token_ref,
    next_three_ref, next_dot_ref,
):
    def run(up_ref, down_ref, up1_ref, down1_ref):
        def one_head(h):
            lanes = head_lanes(h)
            _, grad_scores, _, _ = pair_core(
                up1_ref, [(down_ref, rows_for_query(bias_ref, 1))], lanes
            )
            dq_ref[:, lanes] = dq_in[:, lanes] + dot_tn(grad_scores, up1_ref[FIRST, lanes])
            weights, grad_scores, queries, cotangents = pair_core(
                up_ref, [(down1_ref, rows_for_key(bias_ref, 1))], lanes
            )
            dk_ref[:, lanes] = dk_in[:, lanes] + dot_nn(grad_scores, queries)
            dv_ref[:, lanes] = dv_in[:, lanes] + dot_nn(weights, cotangents)
            log_row, dot_row = stat_rows(down1_ref, lanes)
            next_three_ref[:, lanes] = with_bias(as_column(log_row), by_query(bias_ref, 2))
            next_dot_ref[:, lanes] = as_column(dot_row)

        over_heads(one_head)

    by_parity(run, (a_ref, b_ref, 0), (a1_ref, b1_ref, 1))
    token_ref[...] = jnp.zeros(token_ref.shape, f32)


def terms_kernel(
    copies, a_ref, b_ref, a1_ref, b1_ref, a2_ref, b2_ref, dq_in, dk_ref,
    query_unit_ref, key_unit_ref, gains_ref, two_ref, dot_ref, next_three_ref, next_dot_ref,
    dq_ref, terms_ref,
):
    def run(up_ref, down_ref, up1_ref, down1_ref, up2_ref, down2_ref):
        def one_head(h, sums):
            lanes = head_lanes(h)
            parts, queries = grad_query_core(
                up2_ref,
                [(down_ref, two_ref, dot_ref), (down1_ref, next_three_ref, next_dot_ref)],
                lanes,
            )
            total = dq_in[:, lanes] + parts[:CAP]
            dq_ref[:, lanes] = total
            products = parts * queries.astype(f32)
            return (
                sums[0] + jnp.sum(total * query_unit_ref[:, lanes], axis=0, keepdims=True),
                sums[1]
                + jnp.sum(dk_ref[:, lanes] * key_unit_ref[:, lanes], axis=0, keepdims=True),
                sums[2] + jnp.sum(products[:CAP], axis=0, keepdims=True),
                sums[3] + jnp.sum(products[CAP:], axis=0, keepdims=True),
            )

        none = jnp.zeros((1, WIDTH), f32)
        for_query, for_key, two, three = lax.fori_loop(0, HEADS, one_head, (none,) * 4, unroll=HEADS)
        for_query = for_query + three / gains_ref[0:1]
        for_key = for_key + (two + three) / gains_ref[1:2]
        both = jnp.concatenate([for_query, for_key], axis=0) * SCALE
        terms_ref[...] = jnp.broadcast_to(both[None], (copies, 2, WIDTH))

    by_parity(run, (a_ref, b_ref, 0), (a1_ref, b1_ref, 1), (a2_ref, b2_ref, 2))


def norm_back(total, unit, inverse, gain):
    scaled = total * (gain * SCALE)
    return (inverse * (scaled - unit * jnp.mean(scaled * unit, axis=-1, keepdims=True))).astype(bf16)


def last_kernel(
    a_hbm, b_hbm, a2_hbm, b2_hbm, a3_hbm, b3_hbm, bias_hbm, gains_hbm,
    dq_hbm, dk_hbm, dv_hbm, query_unit_hbm, query_inverse_hbm, key_unit_hbm, key_inverse_hbm,
    three_hbm, dot_hbm, sums_ref,
    query_grad_ref, key_grad_ref, value_grad_ref, token_ref,
    *scratch,
):
    (
        up_ref, down_ref, down2_ref, up3_ref, down3_ref,
        dq_in, dk_in, dv_in, query_unit_ref, query_inverse_ref, key_unit_ref, key_inverse_ref,
        three_ref, dot_ref, bias_ref, gains_ref, sems,
    ) = scratch
    token_ref[...] = jnp.zeros(token_ref.shape, f32)

    def run(up_hbm, down_hbm, up2_hbm, down2_hbm, up3_hbm, down3_hbm):
        small = [
            pltpu.make_async_copy(bias_hbm, bias_ref, sems.at[LAST_GROUPS, 0]),
            pltpu.make_async_copy(gains_hbm, gains_ref, sems.at[LAST_GROUPS, 1]),
        ]
        wide = [
            (up_hbm, up_ref), (down_hbm, down_ref), (up3_hbm, up3_ref),
            (three_hbm, three_ref), (dot_hbm, dot_ref), (dq_hbm, dq_in),
            (query_unit_hbm, query_unit_ref), (query_inverse_hbm, query_inverse_ref),
            (down2_hbm, down2_ref), (down3_hbm, down3_ref), (dk_hbm, dk_in),
            (key_unit_hbm, key_unit_ref), (key_inverse_hbm, key_inverse_ref), (dv_hbm, dv_in),
        ]
        each = HEADS // LAST_GROUPS
        moves = []
        for group in range(LAST_GROUPS):
            lanes = slice(group * each * WIDTH, (group + 1) * each * WIDTH)
            moves.append(
                [
                    pltpu.make_async_copy(hbm.at[:, lanes], ref.at[:, lanes], sems.at[group, i])
                    for i, (hbm, ref) in enumerate(wide)
                ]
            )
        for move in small + sum(moves, []):
            move.start()
        for move in small:
            move.wait()

        def one_head(h):
            lanes = slice(h * WIDTH, (h + 1) * WIDTH)
            part, _ = grad_query_core(up3_ref, [(down_ref, three_ref, dot_ref)], lanes)
            total = dq_in[:, lanes] + part
            query_grad_ref[0, :, lanes] = norm_back(
                total, query_unit_ref[:, lanes], query_inverse_ref[:, lanes], gains_ref[0:1]
            )
            weights, grad_scores, queries, cotangents = pair_core(
                up_ref,
                [(down2_ref, rows_for_key(bias_ref, 2)), (down3_ref, rows_for_key(bias_ref, 3))],
                lanes,
            )
            total = dk_in[:, lanes] + dot_nn(grad_scores, queries)
            key_grad_ref[0, :, lanes] = norm_back(
                total, key_unit_ref[:, lanes], key_inverse_ref[:, lanes], gains_ref[1:2]
            )
            total = dv_in[:, lanes] + dot_nn(weights, cotangents)
            value_grad_ref[0, :, lanes] = total.astype(bf16)

        for group in range(LAST_GROUPS):
            for move in moves[group]:
                move.wait()
            for h in range(group * each, (group + 1) * each):
                one_head(h)

    by_parity(run, (a_hbm, b_hbm, 0), (a2_hbm, b2_hbm, 2), (a3_hbm, b3_hbm, 3))


def sum_kernel(parts_ref, out_ref):
    total = jnp.sum(parts_ref[...], axis=0)
    out_ref[...] = jnp.broadcast_to(total[None], out_ref.shape)


def total_kernel(divisor, parts_ref, token_ref, query_gain_grad_ref, key_gain_grad_ref):
    total = jnp.sum(parts_ref[...], axis=0) / divisor
    query_gain_grad_ref[...] = total[0:1]
    key_gain_grad_ref[...] = total[1:2]


def tie_kernel(chain_ref, token_ref, out_ref, *given):
    for ref in given:
        ref[...] = jnp.zeros(ref.shape, ref.dtype)


VMEM = pl.BlockSpec(memory_space=pltpu.VMEM)
SMEM = pl.BlockSpec(memory_space=pltpu.SMEM)
ANY = pl.BlockSpec(memory_space=pl.ANY)
HBM = pl.BlockSpec(memory_space=pltpu.HBM)


def call(kernel, outs, specs, operands, aliases=None, scratch=(), limit=16 << 20):
    return pl.pallas_call(
        kernel,
        out_shape=tuple(outs),
        in_specs=specs,
        out_specs=(VMEM,) * len(outs),
        scratch_shapes=list(scratch),
        input_output_aliases=aliases or {},
        cost_estimate=pl.CostEstimate(flops=1 << 29, bytes_accessed=1 << 20, transcendentals=0),
        compiler_params=pltpu.CompilerParams(vmem_limit_bytes=limit),
    )(*operands)


def after(chain, token):
    return pl.pallas_call(
        tie_kernel,
        out_shape=jax.ShapeDtypeStruct(chain.shape, chain.dtype),
        in_specs=[ANY, ANY],
        out_specs=ANY,
        input_output_aliases={0: 0},
        compiler_params=pltpu.CompilerParams(vmem_limit_bytes=1 << 20),
    )(chain, token)


def swapped(value, odd):
    count = lax.axis_size("tm")
    pairs = [(i, (i + 1 if i % 2 == odd else i - 1) % count) for i in range(count)]
    return lax.ppermute(value, "tm", pairs)


def body(
    query_raw, key_raw, value_rows, grad_output, log_normalizer, output_dot,
    query_gain, key_gain, route_blocks, route_count, query_reach,
):
    shards, clips = lax.axis_size("tm"), lax.axis_size("dp")
    qgain, kgain = query_gain[None], key_gain[None]

    def like(rows, dtype):
        return jax.ShapeDtypeStruct((rows, HD), dtype)

    total, wide = like(CAP, f32), like(ROWS, bf16)
    lines = jax.ShapeDtypeStruct((24, CAP), f32)
    a, b = call(
        prep_kernel,
        (wide, wide),
        [HBM] * 8,
        (
            query_raw, key_raw, value_rows, grad_output,
            jnp.swapaxes(log_normalizer, 0, 1), jnp.swapaxes(output_dot, 0, 1), qgain, kgain,
        ),
        scratch=(
            pltpu.VMEM((CAP, HD), bf16), pltpu.VMEM((CAP, HD), bf16),
            pltpu.VMEM((HEADS, 1, CAP), f32), pltpu.VMEM((HEADS, 1, CAP), f32),
            pltpu.VMEM((1, WIDTH), f32), pltpu.VMEM((1, WIDTH), f32),
            pltpu.SemaphoreType.DMA((8,)),
        ),
        limit=62 << 20,
    )
    a1, b1 = swapped(a, 0), swapped(b, 1)
    dq, dk, dv, bias, *units, two, three, dots, gains = call(
        own_kernel,
        (total, total, total, lines) + (total,) * 7 + (jax.ShapeDtypeStruct((2, WIDTH), f32),),
        [SMEM] * 3 + [VMEM] * 6,
        (
            jnp.swapaxes(route_blocks, 1, 2), route_count, query_reach,
            a, b, query_raw, key_raw, qgain, kgain,
        ),
    )
    a1 = after(a1, bias)
    a2, b2 = swapped(a1, 1), swapped(b1, 0)
    dq, dk, dv, token, next_three, next_dots = call(
        step_kernel,
        (total, total, total, lines, total, total),
        [VMEM] * 8,
        (a, b, a1, b1, bias, dq, dk, dv),
        {5: 0, 6: 1, 7: 2},
    )
    b2 = after(b2, token)
    b3, a3 = swapped(b2, 1), swapped(a2, 0)
    ends = 2 if clips % 4 == 0 else 1
    first = [
        [clip for clip in range(clips) if clip // 2 % ends == end] for end in range(ends)
    ]
    second = [
        [shard * clips + clip for shard in range(shards) for clip in column]
        for column in zip(*first)
    ]
    dq, terms = call(
        functools.partial(terms_kernel, len(first[0])),
        (total, jax.ShapeDtypeStruct((len(first[0]), 2, WIDTH), f32)),
        [VMEM] * 15,
        (
            a, b, a1, b1, a2, b2, dq, dk, units[0], units[2], gains,
            two, dots, next_three, next_dots,
        ),
        {6: 0},
    )
    parts = lax.all_to_all(terms, "dp", 0, 0, axis_index_groups=first)
    (sums,) = call(
        sum_kernel, (jax.ShapeDtypeStruct((len(second[0]), 2, WIDTH), f32),), [VMEM], (parts,)
    )
    parts = lax.all_to_all(sums, ("tm", "dp"), 0, 0, axis_index_groups=second)
    row = jax.ShapeDtypeStruct((1, CAP, HD), bf16)
    query_grad, key_grad, value_grad, token = call(
        last_kernel,
        (row, row, row, jax.ShapeDtypeStruct((8, WIDTH), f32)),
        [HBM] * 17 + [VMEM],
        (a, b, a2, b2, a3, b3, bias, gains, dq, dk, dv, *units, three, dots, sums),
        scratch=[pltpu.VMEM((ROWS, HD), bf16)] * 5 + [pltpu.VMEM((CAP, HD), f32)] * 9
        + [pltpu.VMEM((24, CAP), f32), pltpu.VMEM((2, WIDTH), f32)]
        + [pltpu.SemaphoreType.DMA((LAST_GROUPS + 1, 14))],
        limit=LAST_LIMIT,
    )
    gain = jax.ShapeDtypeStruct((1, WIDTH), f32)
    query_gain_grad, key_gain_grad = call(
        functools.partial(total_kernel, shards * clips),
        (gain, gain),
        [VMEM, VMEM],
        (parts, token),
        limit=1 << 20,
    )
    return (query_grad, key_grad, value_grad, query_gain_grad[0], key_gain_grad[0])


def solution(mesh):
    rows = P("dp", "tm", None)
    stats = P("dp", None, "tm")
    return jax.shard_map(
        body,
        mesh=mesh,
        in_specs=(
            rows, rows, rows, rows, stats, stats, P(), P(),
            P("dp", None, None), P("dp", None), P("dp", None),
        ),
        out_specs=(rows, rows, rows, P(), P()),
        check_vma=False,
    )
```

```python
import functools

import jax
import jax.numpy as jnp
from jax import lax
from jax.experimental import pallas as pl
from jax.experimental.pallas import tpu as pltpu
from jax.sharding import PartitionSpec as P

BLK = 64
NBLK = 3
ROUTE_MOST = 2
STEPS = 4
HEADS = 12
WIDTH = 128
CAP = ROUTE_MOST * BLK
HD = HEADS * WIDTH
STAT_ROWS = 16
ROWS = 2 * CAP + STAT_ROWS
FIRST, SECOND, STATS = slice(0, CAP), slice(CAP, 2 * CAP), slice(2 * CAP, ROWS)
LOG2E = 1.4426950408889634
SCALE = WIDTH**-0.5
CLOSED = -1e30
norm_eps = 1e-06
LAST_GROUPS = 3
LAST_LIMIT = 60 << 20

f32 = jnp.float32
bf16 = jnp.bfloat16


def head_lanes(h):
    return pl.ds(pl.multiple_of(h * WIDTH, WIDTH), WIDTH)


def over_heads(step, unroll=HEADS):
    lax.fori_loop(0, HEADS, lambda h, none: step(h), None, unroll=unroll)


def by_parity(run, *chains):
    odd = lax.rem(lax.axis_index("tm"), 2)
    for parity in range(2):
        refs = []
        for a, b, hop in chains:
            refs += [a, b] if (parity + hop) % 2 == 0 else [b, a]

        @pl.when(odd == parity)
        def _():
            run(*refs)


def unit_of(raw):
    widened = raw.astype(f32)
    inverse = lax.rsqrt(jnp.mean(widened * widened, axis=-1, keepdims=True) + norm_eps)
    return widened * inverse, inverse


def three_parts(row):
    high = row.astype(bf16)
    rest = row - high.astype(f32)
    middle = rest.astype(bf16)
    low = (rest - middle.astype(f32)).astype(bf16)
    return high, middle, low


def prep_kernel(
    query_hbm, key_hbm, value_hbm, grad_hbm, log_hbm, dot_hbm, qgain_hbm, kgain_hbm,
    a_hbm, b_hbm,
    *scratch,
):
    by_parity(
        lambda up_hbm, down_hbm: prepare(
            query_hbm, key_hbm, value_hbm, grad_hbm, log_hbm, dot_hbm, qgain_hbm, kgain_hbm,
            up_hbm, down_hbm,
            *scratch,
        ),
        (a_hbm, b_hbm, 0),
    )


def prepare(
    query_hbm, key_hbm, value_hbm, grad_hbm, log_hbm, dot_hbm, qgain_hbm, kgain_hbm,
    up_hbm, down_hbm,
    query_ref, key_ref, log_ref, dot_ref, qgain_ref, kgain_ref, up_ref, down_ref, sems,
):
    moves = [
        pltpu.make_async_copy(source, target, sems.at[i])
        for i, (source, target) in enumerate(
            [
                (query_hbm.at[0], query_ref),
                (log_hbm, log_ref),
                (dot_hbm, dot_ref),
                (qgain_hbm, qgain_ref),
                (kgain_hbm, kgain_ref),
                (key_hbm.at[0], key_ref),
                (grad_hbm.at[0], down_ref.at[SECOND]),
                (value_hbm.at[0], up_ref.at[SECOND]),
            ]
        )
    ]
    for move in moves:
        move.start()
    for move in moves[:6]:
        move.wait()

    def one_head(h):
        lanes = slice(h * WIDTH, (h + 1) * WIDTH)
        unit, _ = unit_of(query_ref[:, lanes])
        down_ref[FIRST, lanes] = (unit * qgain_ref[...]).astype(bf16)
        unit, _ = unit_of(key_ref[:, lanes])
        up_ref[FIRST, lanes] = (unit * kgain_ref[...]).astype(bf16)
        parts = [
            p.astype(f32) for p in three_parts(log_ref[h] * -LOG2E) + three_parts(dot_ref[h])
        ]
        parts.append(jnp.zeros((STAT_ROWS - len(parts), CAP), f32))
        down_ref[STATS, lanes] = jnp.concatenate(parts, axis=0).astype(bf16)
        up_ref[STATS, lanes] = jnp.zeros((STAT_ROWS, CAP), bf16)

    each = HEADS // LAST_GROUPS
    sent = []
    for group in range(LAST_GROUPS):
        for h in range(group * each, (group + 1) * each):
            one_head(h)
        if group == 0:
            for move in moves[6:]:
                move.wait()
        lanes = slice(group * each * WIDTH, (group + 1) * each * WIDTH)
        for i, (ref, hbm) in enumerate([(up_ref, up_hbm), (down_ref, down_hbm)]):
            move = pltpu.make_async_copy(
                ref.at[:, lanes], hbm.at[:, lanes], sems.at[8 + 2 * group + i]
            )
            move.start()
            sent.append(move)
    for move in sent:
        move.wait()


def stat_rows(down_ref, lanes):
    stats = down_ref[STATS, lanes].astype(f32)
    return stats[0:1] + stats[1:2] + stats[2:3], stats[3:4] + stats[4:5] + stats[5:6]


def dot_nt(a, b):
    return lax.dot_general(a, b, (((1,), (1,)), ((), ())), preferred_element_type=f32)


def dot_nn(a, b):
    return lax.dot_general(a, b, (((1,), (0,)), ((), ())), preferred_element_type=f32)


def dot_tn(a, b):
    return lax.dot_general(a, b, (((0,), (0,)), ((), ())), preferred_element_type=f32)


def side_by_side(parts, axis):
    return parts[0] if len(parts) == 1 else jnp.concatenate(parts, axis=axis)


def pair_core(up_ref, downs, lanes):
    logs, dots = zip(*(stat_rows(ref, lanes) for ref, _ in downs))
    queries = side_by_side([ref[FIRST, lanes] for ref, _ in downs], 0)
    cotangents = side_by_side([ref[SECOND, lanes] for ref, _ in downs], 0)
    scores = dot_nt(up_ref[FIRST, lanes], queries)
    half = []
    for j in range(ROUTE_MOST):
        row = side_by_side([log + bias[j : j + 1] for log, (_, bias) in zip(logs, downs)], 1)
        half.append(jnp.exp2(scores[j * BLK : (j + 1) * BLK] * (SCALE * LOG2E) + row))
    probability = jnp.concatenate(half, axis=0)
    grad_weights = dot_nt(up_ref[SECOND, lanes], cotangents)
    grad_scores = (probability * (grad_weights - side_by_side(dots, 1))).astype(bf16)
    return probability.astype(bf16), grad_scores, queries, cotangents


def rows_for_query(bias_ref, offset):
    return bias_ref[offset * ROUTE_MOST : (offset + 1) * ROUTE_MOST, :]


def rows_for_key(bias_ref, offset):
    return rows_for_query(bias_ref, STEPS - 1 + offset)


def by_query(bias_ref, which):
    at = (2 * STEPS - 1 + which) * ROUTE_MOST
    return bias_ref[at : at + ROUTE_MOST, :]


def as_column(row):
    return jnp.transpose(jnp.broadcast_to(row, (CAP, CAP)))


def with_bias(column, bias):
    return jnp.concatenate(
        [column[i * BLK : (i + 1) * BLK] + bias[i : i + 1] for i in range(ROUTE_MOST)], axis=0
    )


def grad_query_core(up_ref, downs, lanes):
    queries = side_by_side([ref[FIRST, lanes] for ref, _, _ in downs], 0)
    cotangents = side_by_side([ref[SECOND, lanes] for ref, _, _ in downs], 0)
    known = side_by_side([ref[:, lanes] for _, ref, _ in downs], 0)
    dots = side_by_side([ref[:, lanes] for _, _, ref in downs], 0)
    probability = jnp.exp2(dot_nt(queries, up_ref[FIRST, lanes]) * (SCALE * LOG2E) + known)
    grad_weights = dot_nt(cotangents, up_ref[SECOND, lanes])
    grad_scores = (probability * (grad_weights - dots)).astype(bf16)
    return dot_nn(grad_scores, up_ref[FIRST, lanes]), queries


def fill_bias(blocks_ref, counts_ref, reach_ref, bias_ref):
    shards = counts_ref.shape[1]
    here = lax.axis_index("tm")
    lane = lax.broadcasted_iota(jnp.int32, (1, CAP), 1)

    def pair_rows(query_shard, key_shard, offset, by_query=False):
        rows = []
        for outer in range(ROUTE_MOST):
            values = []
            for inner in range(ROUTE_MOST):
                qi, kj = (outer, inner) if by_query else (inner, outer)
                near = (
                    offset * NBLK
                    + blocks_ref[0, qi, query_shard]
                    - blocks_ref[0, kj, key_shard]
                    < reach_ref[0, query_shard * ROUTE_MOST + qi]
                )
                live = (qi < counts_ref[0, query_shard]) & (kj < counts_ref[0, key_shard])
                values.append(jnp.where(near & live, 0.0, CLOSED).astype(f32))
            rows.append(jnp.where(lane < BLK, values[0], values[1]))
        return rows

    rows = []
    for offset in range(STEPS):
        rows += pair_rows(here, lax.rem(here - offset + shards, shards), offset)
    for offset in range(1, STEPS):
        rows += pair_rows(lax.rem(here + offset, shards), here, offset)
    two_back = lax.rem(here - 2 + shards, shards)
    rows += pair_rows(here, two_back, 2, True)
    rows += pair_rows(here, lax.rem(here - 3 + shards, shards), 3, True)
    rows += pair_rows(lax.rem(here + 1, shards), two_back, 3, True)
    rows += [jnp.zeros((1, CAP), f32)] * (bias_ref.shape[0] - len(rows))
    for at, row in enumerate(rows):
        bias_ref[at : at + 1, :] = row


def own_kernel(
    blocks_ref, counts_ref, reach_ref, a_ref, b_ref, query_ref, key_ref, qgain_ref, kgain_ref,
    dq_ref, dk_ref, dv_ref, bias_ref, query_unit_ref, query_inverse_ref, key_unit_ref, key_inverse_ref,
    two_ref, three_ref, dot_ref, gains_ref,
):
    fill_bias(blocks_ref, counts_ref, reach_ref, bias_ref)
    gains_ref[...] = jnp.concatenate([qgain_ref[...], kgain_ref[...]], axis=0)

    def run(up_ref, down_ref):
        def one_head(h):
            lanes = head_lanes(h)
            weights, grad_scores, queries, cotangents = pair_core(
                up_ref, [(down_ref, rows_for_query(bias_ref, 0))], lanes
            )
            dq_ref[:, lanes] = dot_tn(grad_scores, up_ref[FIRST, lanes])
            dk_ref[:, lanes] = dot_nn(grad_scores, queries)
            dv_ref[:, lanes] = dot_nn(weights, cotangents)
            for raw_ref, unit_ref, inverse_ref in (
                (query_ref, query_unit_ref, query_inverse_ref),
                (key_ref, key_unit_ref, key_inverse_ref),
            ):
                unit, inverse = unit_of(raw_ref[0, :, lanes])
                unit_ref[:, lanes] = unit
                inverse_ref[:, lanes] = jnp.broadcast_to(inverse, unit.shape)
            log_row, dot_row = stat_rows(down_ref, lanes)
            column = as_column(log_row)
            two_ref[:, lanes] = with_bias(column, by_query(bias_ref, 0))
            three_ref[:, lanes] = with_bias(column, by_query(bias_ref, 1))
            dot_ref[:, lanes] = as_column(dot_row)

        over_heads(one_head)

    by_parity(run, (a_ref, b_ref, 0))


def step_kernel(
    a_ref, b_ref, a1_ref, b1_ref, bias_ref, dq_in, dk_in, dv_in, dq_ref, dk_ref, dv_ref, token_ref,
    next_three_ref, next_dot_ref,
):
    def run(up_ref, down_ref, up1_ref, down1_ref):
        def one_head(h):
            lanes = head_lanes(h)
            _, grad_scores, _, _ = pair_core(
                up1_ref, [(down_ref, rows_for_query(bias_ref, 1))], lanes
            )
            dq_ref[:, lanes] = dq_in[:, lanes] + dot_tn(grad_scores, up1_ref[FIRST, lanes])
            weights, grad_scores, queries, cotangents = pair_core(
                up_ref, [(down1_ref, rows_for_key(bias_ref, 1))], lanes
            )
            dk_ref[:, lanes] = dk_in[:, lanes] + dot_nn(grad_scores, queries)
            dv_ref[:, lanes] = dv_in[:, lanes] + dot_nn(weights, cotangents)
            log_row, dot_row = stat_rows(down1_ref, lanes)
            next_three_ref[:, lanes] = with_bias(as_column(log_row), by_query(bias_ref, 2))
            next_dot_ref[:, lanes] = as_column(dot_row)

        over_heads(one_head)

    by_parity(run, (a_ref, b_ref, 0), (a1_ref, b1_ref, 1))
    token_ref[...] = jnp.zeros(token_ref.shape, f32)


def terms_kernel(
    copies, a_ref, b_ref, a1_ref, b1_ref, a2_ref, b2_ref, dq_in, dk_ref,
    query_unit_ref, key_unit_ref, gains_ref, two_ref, dot_ref, next_three_ref, next_dot_ref,
    dq_ref, terms_ref,
):
    def run(up_ref, down_ref, up1_ref, down1_ref, up2_ref, down2_ref):
        def one_head(h, sums):
            lanes = head_lanes(h)
            parts, queries = grad_query_core(
                up2_ref,
                [(down_ref, two_ref, dot_ref), (down1_ref, next_three_ref, next_dot_ref)],
                lanes,
            )
            total = dq_in[:, lanes] + parts[:CAP]
            dq_ref[:, lanes] = total
            products = parts * queries.astype(f32)
            return (
                sums[0] + jnp.sum(total * query_unit_ref[:, lanes], axis=0, keepdims=True),
                sums[1]
                + jnp.sum(dk_ref[:, lanes] * key_unit_ref[:, lanes], axis=0, keepdims=True),
                sums[2] + jnp.sum(products[:CAP], axis=0, keepdims=True),
                sums[3] + jnp.sum(products[CAP:], axis=0, keepdims=True),
            )

        none = jnp.zeros((1, WIDTH), f32)
        for_query, for_key, two, three = lax.fori_loop(0, HEADS, one_head, (none,) * 4, unroll=HEADS)
        for_query = for_query + three / gains_ref[0:1]
        for_key = for_key + (two + three) / gains_ref[1:2]
        both = jnp.concatenate([for_query, for_key], axis=0) * SCALE
        terms_ref[...] = jnp.broadcast_to(both[None], (copies, 2, WIDTH))

    by_parity(run, (a_ref, b_ref, 0), (a1_ref, b1_ref, 1), (a2_ref, b2_ref, 2))


def norm_back(total, unit, inverse, gain):
    scaled = total * (gain * SCALE)
    return (inverse * (scaled - unit * jnp.mean(scaled * unit, axis=-1, keepdims=True))).astype(bf16)


def last_kernel(
    a_hbm, b_hbm, a2_hbm, b2_hbm, a3_hbm, b3_hbm, bias_hbm, gains_hbm,
    dq_hbm, dk_hbm, dv_hbm, query_unit_hbm, query_inverse_hbm, key_unit_hbm, key_inverse_hbm,
    three_hbm, dot_hbm, sums_ref,
    query_grad_ref, key_grad_ref, value_grad_ref, token_ref,
    *scratch,
):
    (
        up_ref, down_ref, down2_ref, up3_ref, down3_ref,
        dq_in, dk_in, dv_in, query_unit_ref, query_inverse_ref, key_unit_ref, key_inverse_ref,
        three_ref, dot_ref, bias_ref, gains_ref, sems,
    ) = scratch
    token_ref[...] = jnp.zeros(token_ref.shape, f32)

    def run(up_hbm, down_hbm, up2_hbm, down2_hbm, up3_hbm, down3_hbm):
        small = [
            pltpu.make_async_copy(bias_hbm, bias_ref, sems.at[LAST_GROUPS, 0]),
            pltpu.make_async_copy(gains_hbm, gains_ref, sems.at[LAST_GROUPS, 1]),
        ]
        wide = [
            (up_hbm, up_ref), (down_hbm, down_ref), (up3_hbm, up3_ref),
            (three_hbm, three_ref), (dot_hbm, dot_ref), (dq_hbm, dq_in),
            (query_unit_hbm, query_unit_ref), (query_inverse_hbm, query_inverse_ref),
            (down2_hbm, down2_ref), (down3_hbm, down3_ref), (dk_hbm, dk_in),
            (key_unit_hbm, key_unit_ref), (key_inverse_hbm, key_inverse_ref), (dv_hbm, dv_in),
        ]
        each = HEADS // LAST_GROUPS
        moves = []
        for group in range(LAST_GROUPS):
            lanes = slice(group * each * WIDTH, (group + 1) * each * WIDTH)
            moves.append(
                [
                    pltpu.make_async_copy(hbm.at[:, lanes], ref.at[:, lanes], sems.at[group, i])
                    for i, (hbm, ref) in enumerate(wide)
                ]
            )
        for move in small + sum(moves, []):
            move.start()
        for move in small:
            move.wait()

        def one_head(h):
            lanes = slice(h * WIDTH, (h + 1) * WIDTH)
            part, _ = grad_query_core(up3_ref, [(down_ref, three_ref, dot_ref)], lanes)
            total = dq_in[:, lanes] + part
            query_grad_ref[0, :, lanes] = norm_back(
                total, query_unit_ref[:, lanes], query_inverse_ref[:, lanes], gains_ref[0:1]
            )
            weights, grad_scores, queries, cotangents = pair_core(
                up_ref,
                [(down2_ref, rows_for_key(bias_ref, 2)), (down3_ref, rows_for_key(bias_ref, 3))],
                lanes,
            )
            total = dk_in[:, lanes] + dot_nn(grad_scores, queries)
            key_grad_ref[0, :, lanes] = norm_back(
                total, key_unit_ref[:, lanes], key_inverse_ref[:, lanes], gains_ref[1:2]
            )
            total = dv_in[:, lanes] + dot_nn(weights, cotangents)
            value_grad_ref[0, :, lanes] = total.astype(bf16)

        for group in range(LAST_GROUPS):
            for move in moves[group]:
                move.wait()
            for h in range(group * each, (group + 1) * each):
                one_head(h)

    by_parity(run, (a_hbm, b_hbm, 0), (a2_hbm, b2_hbm, 2), (a3_hbm, b3_hbm, 3))


def sum_kernel(parts_ref, out_ref):
    total = jnp.sum(parts_ref[...], axis=0)
    out_ref[...] = jnp.broadcast_to(total[None], out_ref.shape)


def total_kernel(divisor, parts_ref, token_ref, query_gain_grad_ref, key_gain_grad_ref):
    total = jnp.sum(parts_ref[...], axis=0) / divisor
    query_gain_grad_ref[...] = total[0:1]
    key_gain_grad_ref[...] = total[1:2]


def tie_kernel(chain_ref, token_ref, out_ref, *given):
    for ref in given:
        ref[...] = jnp.zeros(ref.shape, ref.dtype)


VMEM = pl.BlockSpec(memory_space=pltpu.VMEM)
SMEM = pl.BlockSpec(memory_space=pltpu.SMEM)
ANY = pl.BlockSpec(memory_space=pl.ANY)
HBM = pl.BlockSpec(memory_space=pltpu.HBM)


def call(
    kernel, outs, specs, operands, aliases=None, scratch=(), limit=16 << 20, out_spec=None
):
    return pl.pallas_call(
        kernel,
        out_shape=tuple(outs),
        in_specs=specs,
        out_specs=(out_spec or VMEM,) * len(outs),
        scratch_shapes=list(scratch),
        input_output_aliases=aliases or {},
        cost_estimate=pl.CostEstimate(flops=1 << 29, bytes_accessed=1 << 20, transcendentals=0),
        compiler_params=pltpu.CompilerParams(vmem_limit_bytes=limit),
    )(*operands)


def after(chain, token):
    return pl.pallas_call(
        tie_kernel,
        out_shape=jax.ShapeDtypeStruct(chain.shape, chain.dtype),
        in_specs=[ANY, ANY],
        out_specs=ANY,
        input_output_aliases={0: 0},
        compiler_params=pltpu.CompilerParams(vmem_limit_bytes=1 << 20),
    )(chain, token)


def swapped(value, odd):
    count = lax.axis_size("tm")
    pairs = [(i, (i + 1 if i % 2 == odd else i - 1) % count) for i in range(count)]
    return lax.ppermute(value, "tm", pairs)


def body(
    query_raw, key_raw, value_rows, grad_output, log_normalizer, output_dot,
    query_gain, key_gain, route_blocks, route_count, query_reach,
):
    shards, clips = lax.axis_size("tm"), lax.axis_size("dp")
    qgain, kgain = query_gain[None], key_gain[None]

    def like(rows, dtype):
        return jax.ShapeDtypeStruct((rows, HD), dtype)

    total, wide = like(CAP, f32), like(ROWS, bf16)
    lines = jax.ShapeDtypeStruct((24, CAP), f32)
    a, b = call(
        prep_kernel,
        (wide, wide),
        [HBM] * 8,
        (
            query_raw, key_raw, value_rows, grad_output,
            jnp.swapaxes(log_normalizer, 0, 1), jnp.swapaxes(output_dot, 0, 1), qgain, kgain,
        ),
        scratch=(
            pltpu.VMEM((CAP, HD), bf16), pltpu.VMEM((CAP, HD), bf16),
            pltpu.VMEM((HEADS, 1, CAP), f32), pltpu.VMEM((HEADS, 1, CAP), f32),
            pltpu.VMEM((1, WIDTH), f32), pltpu.VMEM((1, WIDTH), f32),
            pltpu.VMEM((ROWS, HD), bf16), pltpu.VMEM((ROWS, HD), bf16),
            pltpu.SemaphoreType.DMA((8 + 2 * LAST_GROUPS,)),
        ),
        limit=62 << 20,
        out_spec=HBM,
    )
    a1, b1 = swapped(a, 0), swapped(b, 1)
    dq, dk, dv, bias, *units, two, three, dots, gains = call(
        own_kernel,
        (total, total, total, lines) + (total,) * 7 + (jax.ShapeDtypeStruct((2, WIDTH), f32),),
        [SMEM] * 3 + [VMEM] * 6,
        (
            jnp.swapaxes(route_blocks, 1, 2), route_count, query_reach,
            a, b, query_raw, key_raw, qgain, kgain,
        ),
    )
    a1 = after(a1, bias)
    a2, b2 = swapped(a1, 1), swapped(b1, 0)
    dq, dk, dv, token, next_three, next_dots = call(
        step_kernel,
        (total, total, total, lines, total, total),
        [VMEM] * 8,
        (a, b, a1, b1, bias, dq, dk, dv),
        {5: 0, 6: 1, 7: 2},
    )
    b2 = after(b2, token)
    b3, a3 = swapped(b2, 1), swapped(a2, 0)
    ends = 2 if clips % 4 == 0 else 1
    first = [
        [clip for clip in range(clips) if clip // 2 % ends == end] for end in range(ends)
    ]
    second = [
        [shard * clips + clip for shard in range(shards) for clip in column]
        for column in zip(*first)
    ]
    dq, terms = call(
        functools.partial(terms_kernel, len(first[0])),
        (total, jax.ShapeDtypeStruct((len(first[0]), 2, WIDTH), f32)),
        [VMEM] * 15,
        (
            a, b, a1, b1, a2, b2, dq, dk, units[0], units[2], gains,
            two, dots, next_three, next_dots,
        ),
        {6: 0},
    )
    parts = lax.all_to_all(terms, "dp", 0, 0, axis_index_groups=first)
    (sums,) = call(
        sum_kernel, (jax.ShapeDtypeStruct((len(second[0]), 2, WIDTH), f32),), [VMEM], (parts,)
    )
    parts = lax.all_to_all(sums, ("tm", "dp"), 0, 0, axis_index_groups=second)
    row = jax.ShapeDtypeStruct((1, CAP, HD), bf16)
    query_grad, key_grad, value_grad, token = call(
        last_kernel,
        (row, row, row, jax.ShapeDtypeStruct((8, WIDTH), f32)),
        [HBM] * 17 + [VMEM],
        (a, b, a2, b2, a3, b3, bias, gains, dq, dk, dv, *units, three, dots, sums),
        scratch=[pltpu.VMEM((ROWS, HD), bf16)] * 5 + [pltpu.VMEM((CAP, HD), f32)] * 9
        + [pltpu.VMEM((24, CAP), f32), pltpu.VMEM((2, WIDTH), f32)]
        + [pltpu.SemaphoreType.DMA((LAST_GROUPS + 1, 14))],
        limit=LAST_LIMIT,
    )
    gain = jax.ShapeDtypeStruct((1, WIDTH), f32)
    query_gain_grad, key_gain_grad = call(
        functools.partial(total_kernel, shards * clips),
        (gain, gain),
        [VMEM, VMEM],
        (parts, token),
        limit=1 << 20,
    )
    return (query_grad, key_grad, value_grad, query_gain_grad[0], key_gain_grad[0])


def solution(mesh):
    rows = P("dp", "tm", None)
    stats = P("dp", None, "tm")
    return jax.shard_map(
        body,
        mesh=mesh,
        in_specs=(
            rows, rows, rows, rows, stats, stats, P(), P(),
            P("dp", None, None), P("dp", None), P("dp", None),
        ),
        out_specs=(rows, rows, rows, P(), P()),
        check_vma=False,
    )
```

```python
import functools

import jax
import jax.numpy as jnp
from jax import lax
from jax.experimental import pallas as pl
from jax.experimental.pallas import tpu as pltpu
from jax.sharding import PartitionSpec as P

BLK = 64
NBLK = 3
ROUTE_MOST = 2
STEPS = 4
HEADS = 12
WIDTH = 128
CAP = ROUTE_MOST * BLK
HD = HEADS * WIDTH
STAT_ROWS = 16
ROWS = 2 * CAP + STAT_ROWS
FIRST, SECOND, STATS = slice(0, CAP), slice(CAP, 2 * CAP), slice(2 * CAP, ROWS)
LOG2E = 1.4426950408889634
SCALE = WIDTH**-0.5
CLOSED = -1e30
norm_eps = 1e-06
LAST_GROUPS = 3
LAST_LIMIT = 60 << 20

f32 = jnp.float32
bf16 = jnp.bfloat16


def head_lanes(h):
    return pl.ds(pl.multiple_of(h * WIDTH, WIDTH), WIDTH)


def over_heads(step, unroll=HEADS):
    lax.fori_loop(0, HEADS, lambda h, none: step(h), None, unroll=unroll)


def by_parity(run, *chains):
    odd = lax.rem(lax.axis_index("tm"), 2)
    for parity in range(2):
        refs = []
        for a, b, hop in chains:
            refs += [a, b] if (parity + hop) % 2 == 0 else [b, a]

        @pl.when(odd == parity)
        def _():
            run(*refs)


def unit_of(raw):
    widened = raw.astype(f32)
    inverse = lax.rsqrt(jnp.mean(widened * widened, axis=-1, keepdims=True) + norm_eps)
    return widened * inverse, inverse


def three_parts(row):
    high = row.astype(bf16)
    rest = row - high.astype(f32)
    middle = rest.astype(bf16)
    low = (rest - middle.astype(f32)).astype(bf16)
    return high, middle, low


def prep_kernel(
    query_hbm, key_hbm, value_hbm, grad_hbm, log_hbm, dot_hbm, qgain_hbm, kgain_hbm,
    a_hbm, b_hbm,
    *scratch,
):
    by_parity(
        lambda up_hbm, down_hbm: prepare(
            query_hbm, key_hbm, value_hbm, grad_hbm, log_hbm, dot_hbm, qgain_hbm, kgain_hbm,
            up_hbm, down_hbm,
            *scratch,
        ),
        (a_hbm, b_hbm, 0),
    )


def prepare(
    query_hbm, key_hbm, value_hbm, grad_hbm, log_hbm, dot_hbm, qgain_hbm, kgain_hbm,
    up_hbm, down_hbm,
    query_ref, key_ref, log_ref, dot_ref, qgain_ref, kgain_ref, up_ref, down_ref, sems,
):
    moves = [
        pltpu.make_async_copy(source, target, sems.at[i])
        for i, (source, target) in enumerate(
            [
                (query_hbm.at[0], query_ref),
                (log_hbm, log_ref),
                (dot_hbm, dot_ref),
                (qgain_hbm, qgain_ref),
                (kgain_hbm, kgain_ref),
                (key_hbm.at[0], key_ref),
                (grad_hbm.at[0], down_ref.at[SECOND]),
                (value_hbm.at[0], up_ref.at[SECOND]),
            ]
        )
    ]
    for move in moves:
        move.start()
    for move in moves[:6]:
        move.wait()

    def one_head(h):
        lanes = slice(h * WIDTH, (h + 1) * WIDTH)
        unit, _ = unit_of(query_ref[:, lanes])
        down_ref[FIRST, lanes] = (unit * qgain_ref[...]).astype(bf16)
        unit, _ = unit_of(key_ref[:, lanes])
        up_ref[FIRST, lanes] = (unit * kgain_ref[...]).astype(bf16)
        parts = [
            p.astype(f32) for p in three_parts(log_ref[h] * -LOG2E) + three_parts(dot_ref[h])
        ]
        parts.append(jnp.zeros((STAT_ROWS - len(parts), CAP), f32))
        down_ref[STATS, lanes] = jnp.concatenate(parts, axis=0).astype(bf16)
        up_ref[STATS, lanes] = jnp.zeros((STAT_ROWS, CAP), bf16)

    each = HEADS // LAST_GROUPS
    sent = []
    for group in range(LAST_GROUPS):
        for h in range(group * each, (group + 1) * each):
            one_head(h)
        if group == 0:
            for move in moves[6:]:
                move.wait()
        lanes = slice(group * each * WIDTH, (group + 1) * each * WIDTH)
        for i, (ref, hbm) in enumerate([(up_ref, up_hbm), (down_ref, down_hbm)]):
            move = pltpu.make_async_copy(
                ref.at[:, lanes], hbm.at[:, lanes], sems.at[8 + 2 * group + i]
            )
            move.start()
            sent.append(move)
    for move in sent:
        move.wait()


def stat_rows(down_ref, lanes):
    stats = down_ref[STATS, lanes].astype(f32)
    return stats[0:1] + stats[1:2] + stats[2:3], stats[3:4] + stats[4:5] + stats[5:6]


def dot_nt(a, b):
    return lax.dot_general(a, b, (((1,), (1,)), ((), ())), preferred_element_type=f32)


def dot_nn(a, b):
    return lax.dot_general(a, b, (((1,), (0,)), ((), ())), preferred_element_type=f32)


def dot_tn(a, b):
    return lax.dot_general(a, b, (((0,), (0,)), ((), ())), preferred_element_type=f32)


def side_by_side(parts, axis):
    return parts[0] if len(parts) == 1 else jnp.concatenate(parts, axis=axis)


def pair_core(up_ref, downs, lanes):
    logs, dots = zip(*(stat_rows(ref, lanes) for ref, _ in downs))
    queries = side_by_side([ref[FIRST, lanes] for ref, _ in downs], 0)
    cotangents = side_by_side([ref[SECOND, lanes] for ref, _ in downs], 0)
    scores = dot_nt(up_ref[FIRST, lanes], queries)
    half = []
    for j in range(ROUTE_MOST):
        row = side_by_side([log + bias[j : j + 1] for log, (_, bias) in zip(logs, downs)], 1)
        half.append(jnp.exp2(scores[j * BLK : (j + 1) * BLK] * (SCALE * LOG2E) + row))
    probability = jnp.concatenate(half, axis=0)
    grad_weights = dot_nt(up_ref[SECOND, lanes], cotangents)
    grad_scores = (probability * (grad_weights - side_by_side(dots, 1))).astype(bf16)
    return probability.astype(bf16), grad_scores, queries, cotangents


def rows_for_query(bias_ref, offset):
    return bias_ref[offset * ROUTE_MOST : (offset + 1) * ROUTE_MOST, :]


def rows_for_key(bias_ref, offset):
    return rows_for_query(bias_ref, STEPS - 1 + offset)


def by_query(bias_ref, which):
    at = (2 * STEPS - 1 + which) * ROUTE_MOST
    return bias_ref[at : at + ROUTE_MOST, :]


def as_column(row):
    return jnp.transpose(jnp.broadcast_to(row, (CAP, CAP)))


def with_bias(column, bias):
    return jnp.concatenate(
        [column[i * BLK : (i + 1) * BLK] + bias[i : i + 1] for i in range(ROUTE_MOST)], axis=0
    )


def grad_query_core(up_ref, downs, lanes):
    queries = side_by_side([ref[FIRST, lanes] for ref, _, _ in downs], 0)
    cotangents = side_by_side([ref[SECOND, lanes] for ref, _, _ in downs], 0)
    known = side_by_side([ref[:, lanes] for _, ref, _ in downs], 0)
    dots = side_by_side([ref[:, lanes] for _, _, ref in downs], 0)
    probability = jnp.exp2(dot_nt(queries, up_ref[FIRST, lanes]) * (SCALE * LOG2E) + known)
    grad_weights = dot_nt(cotangents, up_ref[SECOND, lanes])
    grad_scores = (probability * (grad_weights - dots)).astype(bf16)
    return dot_nn(grad_scores, up_ref[FIRST, lanes]), queries


def fill_bias(blocks_ref, counts_ref, reach_ref, bias_ref):
    shards = counts_ref.shape[1]
    here = lax.axis_index("tm")
    lane = lax.broadcasted_iota(jnp.int32, (1, CAP), 1)

    def pair_rows(query_shard, key_shard, offset, by_query=False):
        rows = []
        for outer in range(ROUTE_MOST):
            values = []
            for inner in range(ROUTE_MOST):
                qi, kj = (outer, inner) if by_query else (inner, outer)
                near = (
                    offset * NBLK
                    + blocks_ref[0, qi, query_shard]
                    - blocks_ref[0, kj, key_shard]
                    < reach_ref[0, query_shard * ROUTE_MOST + qi]
                )
                live = (qi < counts_ref[0, query_shard]) & (kj < counts_ref[0, key_shard])
                values.append(jnp.where(near & live, 0.0, CLOSED).astype(f32))
            rows.append(jnp.where(lane < BLK, values[0], values[1]))
        return rows

    rows = []
    for offset in range(STEPS):
        rows += pair_rows(here, lax.rem(here - offset + shards, shards), offset)
    for offset in range(1, STEPS):
        rows += pair_rows(lax.rem(here + offset, shards), here, offset)
    two_back = lax.rem(here - 2 + shards, shards)
    rows += pair_rows(here, two_back, 2, True)
    rows += pair_rows(here, lax.rem(here - 3 + shards, shards), 3, True)
    rows += pair_rows(lax.rem(here + 1, shards), two_back, 3, True)
    rows += [jnp.zeros((1, CAP), f32)] * (bias_ref.shape[0] - len(rows))
    for at, row in enumerate(rows):
        bias_ref[at : at + 1, :] = row


def own_kernel(
    blocks_ref, counts_ref, reach_ref, a_ref, b_ref, query_ref, key_ref, qgain_ref, kgain_ref,
    dq_ref, dk_ref, dv_ref, bias_ref, query_unit_ref, query_inverse_ref, key_unit_ref, key_inverse_ref,
    two_ref, three_ref, dot_ref, gains_ref,
):
    fill_bias(blocks_ref, counts_ref, reach_ref, bias_ref)
    gains_ref[...] = jnp.concatenate([qgain_ref[...], kgain_ref[...]], axis=0)

    def run(up_ref, down_ref):
        def one_head(h):
            lanes = head_lanes(h)
            weights, grad_scores, queries, cotangents = pair_core(
                up_ref, [(down_ref, rows_for_query(bias_ref, 0))], lanes
            )
            dq_ref[:, lanes] = dot_tn(grad_scores, up_ref[FIRST, lanes])
            dk_ref[:, lanes] = dot_nn(grad_scores, queries)
            dv_ref[:, lanes] = dot_nn(weights, cotangents)
            for raw_ref, unit_ref, inverse_ref in (
                (query_ref, query_unit_ref, query_inverse_ref),
                (key_ref, key_unit_ref, key_inverse_ref),
            ):
                unit, inverse = unit_of(raw_ref[0, :, lanes])
                unit_ref[:, lanes] = unit
                inverse_ref[:, lanes] = jnp.broadcast_to(inverse, unit.shape)
            log_row, dot_row = stat_rows(down_ref, lanes)
            column = as_column(log_row)
            two_ref[:, lanes] = with_bias(column, by_query(bias_ref, 0))
            three_ref[:, lanes] = with_bias(column, by_query(bias_ref, 1))
            dot_ref[:, lanes] = as_column(dot_row)

        over_heads(one_head)

    by_parity(run, (a_ref, b_ref, 0))


def step_kernel(
    a_ref, b_ref, a1_ref, b1_ref, bias_ref, dq_in, dk_in, dv_in, dq_ref, dk_ref, dv_ref, token_ref,
    next_three_ref, next_dot_ref,
):
    def run(up_ref, down_ref, up1_ref, down1_ref):
        def one_head(h):
            lanes = head_lanes(h)
            _, grad_scores, _, _ = pair_core(
                up1_ref, [(down_ref, rows_for_query(bias_ref, 1))], lanes
            )
            dq_ref[:, lanes] = dq_in[:, lanes] + dot_tn(grad_scores, up1_ref[FIRST, lanes])
            weights, grad_scores, queries, cotangents = pair_core(
                up_ref, [(down1_ref, rows_for_key(bias_ref, 1))], lanes
            )
            dk_ref[:, lanes] = dk_in[:, lanes] + dot_nn(grad_scores, queries)
            dv_ref[:, lanes] = dv_in[:, lanes] + dot_nn(weights, cotangents)
            log_row, dot_row = stat_rows(down1_ref, lanes)
            next_three_ref[:, lanes] = with_bias(as_column(log_row), by_query(bias_ref, 2))
            next_dot_ref[:, lanes] = as_column(dot_row)

        over_heads(one_head)

    by_parity(run, (a_ref, b_ref, 0), (a1_ref, b1_ref, 1))
    token_ref[...] = jnp.zeros(token_ref.shape, f32)


def terms_kernel(
    copies, a_ref, b_ref, a1_ref, b1_ref, a2_ref, b2_ref, dq_in, dk_ref,
    query_unit_ref, key_unit_ref, gains_ref, two_ref, dot_ref, next_three_ref, next_dot_ref,
    dq_ref, terms_ref,
):
    def run(up_ref, down_ref, up1_ref, down1_ref, up2_ref, down2_ref):
        def one_head(h, sums):
            lanes = head_lanes(h)
            parts, queries = grad_query_core(
                up2_ref,
                [(down_ref, two_ref, dot_ref), (down1_ref, next_three_ref, next_dot_ref)],
                lanes,
            )
            total = dq_in[:, lanes] + parts[:CAP]
            dq_ref[:, lanes] = total
            products = parts * queries.astype(f32)
            return (
                sums[0] + jnp.sum(total * query_unit_ref[:, lanes], axis=0, keepdims=True),
                sums[1]
                + jnp.sum(dk_ref[:, lanes] * key_unit_ref[:, lanes], axis=0, keepdims=True),
                sums[2] + jnp.sum(products[:CAP], axis=0, keepdims=True),
                sums[3] + jnp.sum(products[CAP:], axis=0, keepdims=True),
            )

        none = jnp.zeros((1, WIDTH), f32)
        for_query, for_key, two, three = lax.fori_loop(0, HEADS, one_head, (none,) * 4, unroll=HEADS)
        for_query = for_query + three / gains_ref[0:1]
        for_key = for_key + (two + three) / gains_ref[1:2]
        both = jnp.concatenate([for_query, for_key], axis=0) * SCALE
        terms_ref[...] = jnp.broadcast_to(both[None], (copies, 2, WIDTH))

    by_parity(run, (a_ref, b_ref, 0), (a1_ref, b1_ref, 1), (a2_ref, b2_ref, 2))


def norm_back(total, unit, inverse, gain):
    scaled = total * (gain * SCALE)
    return (inverse * (scaled - unit * jnp.mean(scaled * unit, axis=-1, keepdims=True))).astype(bf16)


def last_kernel(
    a_hbm, b_hbm, a2_hbm, b2_hbm, a3_hbm, b3_hbm, bias_hbm, gains_hbm,
    dq_hbm, dk_hbm, dv_hbm, query_unit_hbm, query_inverse_hbm, key_unit_hbm, key_inverse_hbm,
    three_hbm, dot_hbm, sums_ref,
    query_grad_ref, key_grad_ref, value_grad_ref, token_ref,
    *scratch,
):
    (
        up_ref, down_ref, down2_ref, up3_ref, down3_ref,
        dq_in, dk_in, dv_in, query_unit_ref, query_inverse_ref, key_unit_ref, key_inverse_ref,
        three_ref, dot_ref, bias_ref, gains_ref, sems,
    ) = scratch
    token_ref[...] = jnp.zeros(token_ref.shape, f32)

    def run(up_hbm, down_hbm, up2_hbm, down2_hbm, up3_hbm, down3_hbm):
        small = [
            pltpu.make_async_copy(bias_hbm, bias_ref, sems.at[LAST_GROUPS, 0]),
            pltpu.make_async_copy(gains_hbm, gains_ref, sems.at[LAST_GROUPS, 1]),
        ]
        wide = [
            (up_hbm, up_ref), (down_hbm, down_ref), (up3_hbm, up3_ref),
            (three_hbm, three_ref), (dot_hbm, dot_ref), (dq_hbm, dq_in),
            (query_unit_hbm, query_unit_ref), (query_inverse_hbm, query_inverse_ref),
            (down2_hbm, down2_ref), (down3_hbm, down3_ref), (dk_hbm, dk_in),
            (key_unit_hbm, key_unit_ref), (key_inverse_hbm, key_inverse_ref), (dv_hbm, dv_in),
        ]
        each = HEADS // LAST_GROUPS
        moves = []
        for group in range(LAST_GROUPS):
            lanes = slice(group * each * WIDTH, (group + 1) * each * WIDTH)
            moves.append(
                [
                    pltpu.make_async_copy(hbm.at[:, lanes], ref.at[:, lanes], sems.at[group, i])
                    for i, (hbm, ref) in enumerate(wide)
                ]
            )
        for move in small + sum(moves, []):
            move.start()
        for move in small:
            move.wait()

        def one_head(h):
            lanes = slice(h * WIDTH, (h + 1) * WIDTH)
            part, _ = grad_query_core(up3_ref, [(down_ref, three_ref, dot_ref)], lanes)
            total = dq_in[:, lanes] + part
            query_grad_ref[0, :, lanes] = norm_back(
                total, query_unit_ref[:, lanes], query_inverse_ref[:, lanes], gains_ref[0:1]
            )
            weights, grad_scores, queries, cotangents = pair_core(
                up_ref,
                [(down2_ref, rows_for_key(bias_ref, 2)), (down3_ref, rows_for_key(bias_ref, 3))],
                lanes,
            )
            total = dk_in[:, lanes] + dot_nn(grad_scores, queries)
            key_grad_ref[0, :, lanes] = norm_back(
                total, key_unit_ref[:, lanes], key_inverse_ref[:, lanes], gains_ref[1:2]
            )
            total = dv_in[:, lanes] + dot_nn(weights, cotangents)
            value_grad_ref[0, :, lanes] = total.astype(bf16)

        for group in range(LAST_GROUPS):
            for move in moves[group]:
                move.wait()
            for h in range(group * each, (group + 1) * each):
                one_head(h)

    by_parity(run, (a_hbm, b_hbm, 0), (a2_hbm, b2_hbm, 2), (a3_hbm, b3_hbm, 3))


def sum_kernel(parts_ref, out_ref):
    total = jnp.sum(parts_ref[...], axis=0)
    out_ref[...] = jnp.broadcast_to(total[None], out_ref.shape)


def total_kernel(divisor, parts_ref, token_ref, query_gain_grad_ref, key_gain_grad_ref):
    total = jnp.sum(parts_ref[...], axis=0) / divisor
    query_gain_grad_ref[...] = total[0:1]
    key_gain_grad_ref[...] = total[1:2]


def tie_kernel(chain_ref, token_ref, out_ref, *given):
    for ref in given:
        ref[...] = jnp.zeros(ref.shape, ref.dtype)


VMEM = pl.BlockSpec(memory_space=pltpu.VMEM)
SMEM = pl.BlockSpec(memory_space=pltpu.SMEM)
ANY = pl.BlockSpec(memory_space=pl.ANY)
HBM = pl.BlockSpec(memory_space=pltpu.HBM)


def call(
    kernel, outs, specs, operands, aliases=None, scratch=(), limit=16 << 20, out_spec=None
):
    return pl.pallas_call(
        kernel,
        out_shape=tuple(outs),
        in_specs=specs,
        out_specs=(out_spec or VMEM,) * len(outs),
        scratch_shapes=list(scratch),
        input_output_aliases=aliases or {},
        cost_estimate=pl.CostEstimate(flops=1 << 29, bytes_accessed=1 << 20, transcendentals=0),
        compiler_params=pltpu.CompilerParams(vmem_limit_bytes=limit),
    )(*operands)


def after(chain, token):
    return pl.pallas_call(
        tie_kernel,
        out_shape=jax.ShapeDtypeStruct(chain.shape, chain.dtype),
        in_specs=[ANY, ANY],
        out_specs=ANY,
        input_output_aliases={0: 0},
        compiler_params=pltpu.CompilerParams(vmem_limit_bytes=1 << 20),
    )(chain, token)


def swapped(value, odd):
    count = lax.axis_size("tm")
    pairs = [(i, (i + 1 if i % 2 == odd else i - 1) % count) for i in range(count)]
    return lax.ppermute(value, "tm", pairs)


def body(
    query_raw, key_raw, value_rows, grad_output, log_normalizer, output_dot,
    query_gain, key_gain, route_blocks, route_count, query_reach,
):
    shards, clips = lax.axis_size("tm"), lax.axis_size("dp")
    qgain, kgain = query_gain[None], key_gain[None]

    def like(rows, dtype):
        return jax.ShapeDtypeStruct((rows, HD), dtype)

    total, wide = like(CAP, f32), like(ROWS, bf16)
    lines = jax.ShapeDtypeStruct((24, CAP), f32)
    a, b = call(
        prep_kernel,
        (wide, wide),
        [HBM] * 8,
        (
            query_raw, key_raw, value_rows, grad_output,
            jnp.swapaxes(log_normalizer, 0, 1), jnp.swapaxes(output_dot, 0, 1), qgain, kgain,
        ),
        scratch=(
            pltpu.VMEM((CAP, HD), bf16), pltpu.VMEM((CAP, HD), bf16),
            pltpu.VMEM((HEADS, 1, CAP), f32), pltpu.VMEM((HEADS, 1, CAP), f32),
            pltpu.VMEM((1, WIDTH), f32), pltpu.VMEM((1, WIDTH), f32),
            pltpu.VMEM((ROWS, HD), bf16), pltpu.VMEM((ROWS, HD), bf16),
            pltpu.SemaphoreType.DMA((8 + 2 * LAST_GROUPS,)),
        ),
        limit=62 << 20,
        out_spec=HBM,
    )
    a1, b1 = swapped(a, 0), swapped(b, 1)
    dq, dk, dv, bias, *units, two, three, dots, gains = call(
        own_kernel,
        (total, total, total, lines) + (total,) * 7 + (jax.ShapeDtypeStruct((2, WIDTH), f32),),
        [SMEM] * 3 + [VMEM] * 6,
        (
            jnp.swapaxes(route_blocks, 1, 2), route_count, query_reach,
            a, b, query_raw, key_raw, qgain, kgain,
        ),
    )
    a1 = after(a1, bias)
    a2, b2 = swapped(a1, 1), swapped(b1, 0)
    dq, dk, dv, token, next_three, next_dots = call(
        step_kernel,
        (total, total, total, lines, total, total),
        [VMEM] * 8,
        (a, b, a1, b1, bias, dq, dk, dv),
        {5: 0, 6: 1, 7: 2},
    )
    a2 = after(a2, token)
    a3, b3 = swapped(a2, 0), swapped(b2, 1)
    ends = 2 if clips % 4 == 0 else 1
    first = [
        [clip for clip in range(clips) if clip // 2 % ends == end] for end in range(ends)
    ]
    second = [
        [shard * clips + clip for shard in range(shards) for clip in column]
        for column in zip(*first)
    ]
    dq, terms = call(
        functools.partial(terms_kernel, len(first[0])),
        (total, jax.ShapeDtypeStruct((len(first[0]), 2, WIDTH), f32)),
        [VMEM] * 15,
        (
            a, b, a1, b1, a2, b2, dq, dk, units[0], units[2], gains,
            two, dots, next_three, next_dots,
        ),
        {6: 0},
    )
    parts = lax.all_to_all(terms, "dp", 0, 0, axis_index_groups=first)
    (sums,) = call(
        sum_kernel, (jax.ShapeDtypeStruct((len(second[0]), 2, WIDTH), f32),), [VMEM], (parts,)
    )
    parts = lax.all_to_all(sums, ("tm", "dp"), 0, 0, axis_index_groups=second)
    row = jax.ShapeDtypeStruct((1, CAP, HD), bf16)
    query_grad, key_grad, value_grad, token = call(
        last_kernel,
        (row, row, row, jax.ShapeDtypeStruct((8, WIDTH), f32)),
        [HBM] * 17 + [VMEM],
        (a, b, a2, b2, a3, b3, bias, gains, dq, dk, dv, *units, three, dots, sums),
        scratch=[pltpu.VMEM((ROWS, HD), bf16)] * 5 + [pltpu.VMEM((CAP, HD), f32)] * 9
        + [pltpu.VMEM((24, CAP), f32), pltpu.VMEM((2, WIDTH), f32)]
        + [pltpu.SemaphoreType.DMA((LAST_GROUPS + 1, 14))],
        limit=LAST_LIMIT,
    )
    gain = jax.ShapeDtypeStruct((1, WIDTH), f32)
    query_gain_grad, key_gain_grad = call(
        functools.partial(total_kernel, shards * clips),
        (gain, gain),
        [VMEM, VMEM],
        (parts, token),
        limit=1 << 20,
    )
    return (query_grad, key_grad, value_grad, query_gain_grad[0], key_gain_grad[0])


def solution(mesh):
    rows = P("dp", "tm", None)
    stats = P("dp", None, "tm")
    return jax.shard_map(
        body,
        mesh=mesh,
        in_specs=(
            rows, rows, rows, rows, stats, stats, P(), P(),
            P("dp", None, None), P("dp", None), P("dp", None),
        ),
        out_specs=(rows, rows, rows, P(), P()),
        check_vma=False,
    )
```
